32 devices in a mesh: parts: 2 (over y), graph: 4 (over z), dp: 2 (over x), tensor: 2 (over core).
Axes of the slice: x: 2, y: 2, z: 4, core: 2. Of those that a mesh axis runs over, the one named last changes fastest.
Arguments:
- edges_in: bfloat16 [4, 4096, 512], P(('parts', 'dp'), 'graph', 'tensor'), parts along dimension 0, may hold values from -6 to 6
- weight: bfloat16 [512, 512], P(None, 'tensor'), may hold values from -0.25 to 0.25
- basis_tiles: bfloat16 [4, 144, 128, 128], P(('parts', 'dp'), 'graph'), parts along dimension 0, may hold values from -0.59765625 to 0.59765625
- target_blocks: int32 [4, 144], P(('parts', 'dp'), 'graph'), parts along dimension 0, may hold values from 0 to 7
- source_blocks: int32 [4, 144], P(('parts', 'dp'), 'graph'), parts along dimension 0, may hold values from 0 to 23
- counts: int32 [4, 4], P(('parts', 'dp'), 'graph'), parts along dimension 0, may hold values from 1 to 36, as said below
- grad_out: bfloat16 [4, 4096, 512], P(('parts', 'dp'), 'graph', 'tensor'), parts along dimension 0, may hold values from -6 to 6
Outputs:
- edges_out: bfloat16 [4, 4096, 512], P(('parts', 'dp'), 'graph', 'tensor'), parts along dimension 0
- grad_edges: bfloat16 [4, 4096, 512], P(('parts', 'dp'), 'graph', 'tensor'), parts along dimension 0
- grad_weight: float32 [1024, 512], P('parts', 'tensor'), parts along dimension 0
The draws below stay inside these ranges and needn't reach their ends.
There are 2 independent parts, one for each index of `parts`. The reference program is written for one: setup_inputs(seed, part) draws one part's arguments, and reference() takes and returns one part's arrays. A program takes and returns all parts, laid end to end along the dimension named above; an argument that names none is the same for every part. Nothing has to cross between parts.
Inputs may be any that keep to these rules, and one draw needn't show every extreme that they name: `counts`: each shard has at least one live slot and some shard of every supercell has all 36 slots live; slots that are not live carry basis values that do not count.
All inputs are finite; a program needn't handle non-finite values.
Results may differ from the reference program's by a relative error of at most 0.0095.
Values may be sent and summed in bfloat16 or wider, within the bound.
No kernel may reach another device: no remote copies, remote signals or barrier semaphores. Data moves between devices by JAX's collectives and lax.ppermute only.
A program may use at most 64 MiB of HBM per device.

```python
import jax
import jax.numpy as jnp
from jax import lax

D = 512
TILE = 128
EB_DEV = 8
TRIP_MAX = 36
SUPERCELLS = 2
SHARDS = 4
EDGES = 4096
TILES = 144


def draw_counts(key, part):
    key = jax.random.fold_in(key, 7)
    first, second = jax.random.split(key)
    spread = jax.random.randint(first, (SUPERCELLS, SHARDS), 0, TRIP_MAX)
    lowest = max(1, TRIP_MAX // 3)
    values = lowest + spread * spread * (TRIP_MAX - lowest) // (TRIP_MAX * TRIP_MAX)
    chosen = jax.random.randint(second, (SUPERCELLS,), 0, SHARDS)
    places = jnp.arange(SHARDS, dtype=jnp.int32)[None, :] == chosen[:, None]
    return jnp.where(places, TRIP_MAX, values).astype(jnp.int32)


def place_ends(drawn, rng, low, top_value):
    index_at = [jax.random.randint(jax.random.fold_in(rng, axis), (), 0, length) for axis, length in enumerate(drawn.shape)]
    main_axis = drawn.shape.index(max(drawn.shape))
    beside = index_at[:main_axis] + [(index_at[main_axis] + 1) % drawn.shape[main_axis]] + index_at[main_axis + 1:]
    return drawn.at[tuple(index_at)].set(low).at[tuple(beside)].set(top_value)


def block_levels(own_key, extent, cuts, least, largest):
    factor_of, own = 1.0, jax.random.fold_in(own_key, 6)
    for dim, parts in cuts:
        heights = jnp.exp(jax.random.uniform(jax.random.fold_in(own, dim), (parts,), jnp.float32, least / len(cuts), largest / len(cuts)))
        factor_of = factor_of * jnp.repeat(heights, extent[dim] // parts).reshape([-1 if axis == dim else 1 for axis in range(len(extent))])
    return factor_of


def gaussian(stream_key, shape, deviation, reach, pieces=(), held_as=jnp.bfloat16):
    level = block_levels(stream_key, shape, pieces, -0.22, 0.18) if pieces else 1.0
    result = jax.random.normal(stream_key, shape, jnp.float32) * deviation * level
    return jnp.minimum(jnp.maximum(result, -reach), reach).astype(held_as)


def setup_inputs(seed: int = 0, part: int = 0) -> dict:
    key_of = jax.random.split(jax.random.key(seed), 8)
    part_keys = jax.random.split(jax.random.fold_in(key_of[7], part), 8)
    edges_in = gaussian(part_keys[0], (SUPERCELLS, EDGES, D), 1.0, 6.0, ((0, 2), (1, 4), (2, 2)))
    weight = gaussian(key_of[1], (D, D), D ** -0.5, 0.25, ((1, 2),))
    basis_tiles = gaussian(part_keys[2], (SUPERCELLS, TILES, TILE, TILE), 0.1, 0.59765625, ((0, 2), (1, 4)))
    target_blocks = place_ends(jax.random.randint(part_keys[3], (SUPERCELLS, TILES), 0, EB_DEV), jax.random.fold_in(part_keys[3], 1), 0, EB_DEV - 1).astype(jnp.int32)
    source_blocks = place_ends(jax.random.randint(part_keys[4], (SUPERCELLS, TILES), 0, 3 * EB_DEV), jax.random.fold_in(part_keys[4], 1), 0, (3 * EB_DEV) - 1).astype(jnp.int32)
    counts = draw_counts(jax.random.fold_in(jax.random.fold_in(key_of[7], part), 71), part)
    grad_out = gaussian(part_keys[6], (SUPERCELLS, EDGES, D), 1.0, 6.0, ((0, 2), (1, 4), (2, 2)))
    return {"edges_in": edges_in, "weight": weight, "basis_tiles": basis_tiles, "target_blocks": target_blocks, "source_blocks": source_blocks, "counts": counts, "grad_out": grad_out}


def slope_factor(preact):
    sig = jax.nn.sigmoid(preact)
    return sig * (1.0 + preact * (1.0 - sig))

def reference(edges_in, weight, basis_tiles, target_blocks, source_blocks, counts, grad_out):
    nblocks = EB_DEV * SHARDS

    def one_cell(items):
        x_rows, tiles, target, source, count_row, g_rows = items
        shard = jnp.arange(TILES, dtype=jnp.int32) // TRIP_MAX
        live = (jnp.arange(TILES, dtype=jnp.int32) % TRIP_MAX < count_row[shard]).astype(jnp.float32)
        tgt = (shard * EB_DEV + target).astype(jnp.int32)
        src = ((shard * EB_DEV - EB_DEV + source) % nblocks).astype(jnp.int32)
        preact = jnp.dot(x_rows, weight, preferred_element_type=jnp.float32)
        activated = jax.nn.silu(preact).astype(jnp.bfloat16)
        tiles_f = tiles.astype(jnp.float32)
        picked = activated.reshape(nblocks, TILE, D)[src].astype(jnp.float32)
        contrib = jnp.einsum('kij,kjc->kic', tiles_f, picked) * live[:, None, None]
        triplet = jnp.zeros((nblocks, TILE, D), jnp.float32).at[tgt].add(contrib).reshape(EDGES, D)
        out_rows = (x_rows.astype(jnp.float32) + triplet).astype(jnp.bfloat16)
        g_picked = g_rows.reshape(nblocks, TILE, D)[tgt].astype(jnp.float32)
        back_terms = jnp.einsum('kji,kjc->kic', tiles_f, g_picked) * live[:, None, None]
        back = jnp.zeros((nblocks, TILE, D), jnp.float32).at[src].add(back_terms).reshape(EDGES, D)
        slope = (back * slope_factor(preact)).astype(jnp.bfloat16)
        grad_rows = (g_rows.astype(jnp.float32) + jnp.dot(slope, weight.T, preferred_element_type=jnp.float32)).astype(jnp.bfloat16)
        weight_part = jnp.dot(x_rows.T, slope, preferred_element_type=jnp.float32)
        return (out_rows, grad_rows, weight_part)
    edges_out, grad_edges, weight_parts = lax.map(one_cell, (edges_in, basis_tiles, target_blocks, source_blocks, counts, grad_out))
    grad_weight = lax.optimization_barrier(jnp.sum(weight_parts, axis=0)) / jnp.sqrt(jnp.float32(SUPERCELLS * EDGES))
    return (edges_out, grad_edges, grad_weight)
```

```python
import functools

import jax
import jax.numpy as jnp
from jax import lax
from jax.experimental import pallas as pl
from jax.experimental.pallas import tpu as pltpu
from jax.sharding import PartitionSpec as P

F32 = jnp.float32
BF16 = jnp.bfloat16
UNROLL = 4
VMEM = pl.BlockSpec(memory_space=pltpu.VMEM)
SMEM = pl.BlockSpec(memory_space=pltpu.SMEM)


def call(body, ins, outs, scratch=(), flops=0, nbytes=0):
    return pl.pallas_call(
        body,
        in_specs=[SMEM if x.dtype == jnp.int32 else VMEM for x in ins],
        out_shape=[jax.ShapeDtypeStruct(s, d) for s, d in outs],
        out_specs=[VMEM for _ in outs],
        scratch_shapes=list(scratch),
        cost_estimate=pl.CostEstimate(flops=flops, bytes_accessed=nbytes, transcendentals=0),
        compiler_params=pltpu.CompilerParams(vmem_limit_bytes=32 * 1024 * 1024),
    )(*ins)


def shift(value, axis, steps):
    count = lax.axis_size(axis)
    return lax.ppermute(value, axis, [(i, (i + steps) % count) for i in range(count)])


def pick(listed, count, source, low, high):
    slots = source.shape[1]

    def step(k, found):
        listed[found] = k
        s = source[0, k]
        inside = (k < count) & (s >= low) & (s < high)
        return found + inside.astype(jnp.int32)

    found = lax.fori_loop(0, slots, step, jnp.int32(0))
    for j in range(UNROLL):
        listed[found + j] = 0
    return found


def over_tiles(listed, found, step):
    def some(i, carry):
        for j in range(UNROLL):
            at = i * UNROLL + j
            step(listed[at], at < found)
        return carry

    lax.fori_loop(0, (found + UNROLL - 1) // UNROLL, some, 0)


def back_body(ranges, nblocks, counts, target, source, tiles, grads, *rest):
    n = len(ranges)
    outs, acc, listed = rest[:n], rest[n], rest[n + 1]
    for (low, base), out in zip(ranges, outs):
        acc[...] = jnp.zeros_like(acc)
        found = pick(listed, counts[0, 0], source, low, low + nblocks)

        def step(k, valid):
            at = jnp.where(valid, source[0, k] - low, nblocks)
            acc[at] += lax.dot_general(
                tiles[k], grads[target[0, k]], (((0,), (0,)), ((), ())), preferred_element_type=F32
            )

        over_tiles(listed, found, step)
        for b in range(nblocks):
            out[b] = acc[b].astype(out.dtype)


def triplet_body(low, nblocks, counts, target, source, tiles, rows, start, out, acc, listed):
    for b in range(nblocks):
        acc[b] = start[b].astype(F32)
    found = pick(listed, counts[0, 0], source, low, low + nblocks)

    def step(k, valid):
        at = jnp.where(valid, target[0, k], nblocks)
        s = jnp.where(valid, source[0, k] - low, 0)
        acc[at] += jnp.dot(tiles[k], rows[s], preferred_element_type=F32)

    over_tiles(listed, found, step)
    for b in range(nblocks):
        out[b] = acc[b].astype(out.dtype)


def preact_body(step, mine, theirs, weight, act, factor, flipped):
    rows, chans = mine.shape
    core = lax.axis_index("tensor")
    own = pl.ds(pl.multiple_of(core * chans, chans), chans)
    other = pl.ds(pl.multiple_of((1 - core) * chans, chans), chans)
    for r in range(0, rows, step):
        at = pl.ds(r, step)
        pre = jnp.dot(mine[at], weight[own], preferred_element_type=F32) + jnp.dot(
            theirs[at], weight[other], preferred_element_type=F32
        )
        sig = 1.0 / (1.0 + jnp.exp(-pre))
        act[at] = (pre * sig).astype(BF16)
        factor[at] = sig * (1.0 + pre * (1.0 - sig))
        flipped[own, at] = mine[at].T
        flipped[other, at] = theirs[at].T


def slope_body(step, ndp, back, from_next, from_prev, factor, grads, weight, flipped, *rest):
    to_core, gsum, keep = rest[:3]
    sends = rest[3 : 2 + ndp]
    slope, part = rest[2 + ndp :]
    rows, chans = grads.shape
    core = lax.axis_index("tensor")
    own = pl.ds(pl.multiple_of(core * chans, chans), chans)
    other = pl.ds(pl.multiple_of((1 - core) * chans, chans), chans)
    last = (((1,), (1,)), ((), ()))
    for r in range(0, rows, step):
        at = pl.ds(r, step)
        total = back[at] + from_next[at].astype(F32) + from_prev[at].astype(F32)
        piece = (total * factor[at]).astype(BF16)
        slope[at] = piece
        to_core[at] = lax.dot_general(piece, weight[other], last, preferred_element_type=F32).astype(BF16)
        gsum[at] = grads[at].astype(F32) + lax.dot_general(
            piece, weight[own], last, preferred_element_type=F32
        )
    part[...] = jnp.dot(flipped[...], slope[...], preferred_element_type=F32)
    dp = lax.axis_index("dp")
    size = keep.shape[0]
    keep[...] = part[pl.ds(pl.multiple_of(dp * size, size), size)]
    for j, send in enumerate(sends):
        to = lax.rem(dp + j + 1, ndp)
        send[...] = part[pl.ds(pl.multiple_of(to * size, size), size)].astype(BF16)


def grads_body(gsum, arrived, out):
    out[...] = (gsum[...] + arrived[...].astype(F32)).astype(BF16)


def scatter_body(ndp, nz, kept, *rest):
    arrived = rest[: ndp - 1]
    keep = rest[ndp - 1]
    sends = rest[ndp : ndp + nz - 1]
    part = rest[ndp + nz - 1]
    total = kept[...]
    for ref in arrived:
        total = total + ref[...].astype(F32)
    part[...] = total
    z = lax.axis_index("graph")
    size = keep.shape[0]
    keep[...] = part[pl.ds(pl.multiple_of(z * size, size), size)]
    for j, send in enumerate(sends):
        to = lax.rem(z + j + 1, nz)
        send[...] = part[pl.ds(pl.multiple_of(to * size, size), size)].astype(BF16)


def total_body(scale, nz, kept, *rest):
    total = kept[...]
    for ref in rest[: nz - 1]:
        total = total + ref[...].astype(F32)
    rest[nz - 1][...] = (total * scale).astype(BF16)


def gather_body(axis, count, *refs):
    out = refs[count]
    me = lax.axis_index(axis)
    size = refs[0].shape[0]
    for j in range(count):
        at = lax.rem(me - j + count, count)
        out[pl.ds(pl.multiple_of(at * size, size), size)] = refs[j][...].astype(out.dtype)


def weight_total(keep, sends, scale):
    ndp, nz = lax.axis_size("dp"), lax.axis_size("graph")
    size, chans = keep.shape
    arrived = [shift(s, "dp", j + 1) for j, s in enumerate(sends)]
    part = size // nz
    parts = call(
        functools.partial(scatter_body, ndp, nz),
        [keep, *arrived],
        [((part, chans), F32)] + [((part, chans), BF16)] * (nz - 1),
        [pltpu.VMEM((size, chans), F32)],
    )
    arrived = [shift(s, "graph", j + 1) for j, s in enumerate(parts[1:])]
    (mine,) = call(
        functools.partial(total_body, scale, nz), [parts[0], *arrived], [((part, chans), BF16)]
    )
    arrived = [shift(mine, "graph", j + 1) for j in range(nz - 1)]
    (wide,) = call(
        functools.partial(gather_body, "graph", nz), [mine, *arrived], [((size, chans), BF16)]
    )
    arrived = [shift(wide, "dp", j + 1) for j in range(ndp - 1)]
    (full,) = call(
        functools.partial(gather_body, "dp", ndp), [wide, *arrived], [((size * ndp, chans), F32)]
    )
    return full


def shards(edges_in, weight, basis_tiles, target_blocks, source_blocks, counts, grad_out):
    rows, chans = edges_in.shape[1], edges_in.shape[2]
    tile = basis_tiles.shape[2]
    nblocks = rows // tile
    slots = basis_tiles.shape[1]
    depth = weight.shape[0]
    ndp, nz = lax.axis_size("dp"), lax.axis_size("graph")
    mine, grads, tiles = edges_in[0], grad_out[0], basis_tiles[0]
    blocks = (nblocks, tile, chans)
    flat = (rows, chans)
    index = [counts, target_blocks, source_blocks, tiles]
    work = [pltpu.VMEM((nblocks + 1, tile, chans), F32), pltpu.SMEM((slots + UNROLL,), jnp.int32)]
    unit = 2 * tile * tile * chans * slots // 3

    theirs = shift(mine, "tensor", 1)
    to_prev, to_next = call(
        functools.partial(back_body, ((0, 0), (2 * nblocks, 0)), nblocks),
        [*index, grads.reshape(blocks)],
        [(blocks, BF16), (blocks, BF16)],
        work,
        flops=2 * unit,
        nbytes=4 * rows * chans,
    )
    from_next = shift(to_prev, "graph", -1)
    from_prev = shift(to_next, "graph", 1)
    (back,) = call(
        functools.partial(back_body, ((nblocks, 0),), nblocks),
        [*index, grads.reshape(blocks)],
        [(blocks, F32)],
        work,
        flops=unit,
        nbytes=4 * rows * chans,
    )
    act, factor, flipped = call(
        functools.partial(preact_body, 256),
        [mine, theirs, weight],
        [(flat, BF16), (flat, F32), ((depth, rows), BF16)],
        flops=2 * rows * depth * chans,
        nbytes=8 * rows * chans,
    )
    act_prev = shift(act, "graph", 1)
    act_next = shift(act, "graph", -1)
    (acc,) = call(
        functools.partial(triplet_body, nblocks, nblocks),
        [*index, act.reshape(blocks), mine.reshape(blocks)],
        [(blocks, F32)],
        work,
        flops=unit,
        nbytes=4 * rows * chans,
    )
    size = depth // ndp
    to_core, gsum, keep, *sends = call(
        functools.partial(slope_body, 256, ndp),
        [back.reshape(flat), from_next.reshape(flat), from_prev.reshape(flat), factor, grads, weight, flipped],
        [(flat, BF16), (flat, F32), ((size, chans), F32)] + [((size, chans), BF16)] * (ndp - 1),
        [pltpu.VMEM(flat, BF16), pltpu.VMEM((depth, chans), F32)],
        flops=4 * rows * depth * chans,
        nbytes=8 * rows * chans,
    )
    arrived = shift(to_core, "tensor", 1)
    (grad_edges,) = call(grads_body, [gsum, arrived], [(flat, BF16)], nbytes=8 * rows * chans)
    scale = float(1.0 / (ndp * edges_in.shape[0] * nz * rows) ** 0.5)
    if size % (16 * nz) == 0:
        grad_weight = weight_total(keep, sends, scale)
    else:
        grad_weight = wide_total(keep, sends, scale)
    (acc,) = call(
        functools.partial(triplet_body, 0, nblocks),
        [*index, act_prev.reshape(blocks), acc],
        [(blocks, F32)],
        work,
        flops=unit,
        nbytes=4 * rows * chans,
    )
    (edges_out,) = call(
        functools.partial(triplet_body, 2 * nblocks, nblocks),
        [*index, act_next.reshape(blocks), acc],
        [(blocks, BF16)],
        work,
        flops=unit,
        nbytes=4 * rows * chans,
    )
    return edges_out.reshape(1, rows, chans), grad_edges[None], grad_weight


def wide_total(keep, sends, scale):
    ndp = lax.axis_size("dp")
    total = keep
    for j, s in enumerate(sends):
        total = total + shift(s, "dp", j + 1).astype(F32)
    total = (lax.psum(total, "graph") * scale).astype(BF16)
    return lax.all_gather(total, "dp", axis=0, tiled=True).astype(F32)


def solution(mesh):
    placed = (
        P(("parts", "dp"), "graph", "tensor"),
        P(None, "tensor"),
        P(("parts", "dp"), "graph", None, None),
        P(("parts", "dp"), "graph"),
        P(("parts", "dp"), "graph"),
        P(("parts", "dp"), "graph"),
        P(("parts", "dp"), "graph", "tensor"),
    )
    return jax.shard_map(
        shards,
        mesh=mesh,
        in_specs=placed,
        out_specs=(
            P(("parts", "dp"), "graph", "tensor"),
            P(("parts", "dp"), "graph", "tensor"),
            P("parts", "tensor"),
        ),
        check_vma=False,
    )
```

```python
import functools

import jax
import jax.numpy as jnp
from jax import lax
from jax.experimental import pallas as pl
from jax.experimental.pallas import tpu as pltpu
from jax.sharding import PartitionSpec as P

F32 = jnp.float32
BF16 = jnp.bfloat16
UNROLL = 4
VMEM = pl.BlockSpec(memory_space=pltpu.VMEM)
SMEM = pl.BlockSpec(memory_space=pltpu.SMEM)
HBM = pl.BlockSpec(memory_space=pltpu.HBM)


def call(body, ins, outs, scratch=(), flops=0, nbytes=0, space=None):
    return pl.pallas_call(
        body,
        in_specs=[space or (SMEM if x.dtype == jnp.int32 else VMEM) for x in ins],
        out_shape=[jax.ShapeDtypeStruct(s, d) for s, d in outs],
        out_specs=[VMEM for _ in outs],
        scratch_shapes=list(scratch),
        cost_estimate=pl.CostEstimate(flops=flops, bytes_accessed=nbytes, transcendentals=0),
        compiler_params=pltpu.CompilerParams(vmem_limit_bytes=32 * 1024 * 1024),
    )(*ins)


def shift(value, axis, steps):
    count = lax.axis_size(axis)
    return lax.ppermute(value, axis, [(i, (i + steps) % count) for i in range(count)])


def pick(listed, count, source, low, high):
    slots = source.shape[1]

    def step(k, found):
        listed[found] = k
        s = source[0, k]
        inside = (k < count) & (s >= low) & (s < high)
        return found + inside.astype(jnp.int32)

    found = lax.fori_loop(0, slots, step, jnp.int32(0))
    for j in range(UNROLL):
        listed[found + j] = 0
    return found


def over_tiles(listed, found, step):
    def some(i, carry):
        for j in range(UNROLL):
            at = i * UNROLL + j
            step(listed[at], at < found)
        return carry

    lax.fori_loop(0, (found + UNROLL - 1) // UNROLL, some, 0)


def back_body(ranges, nblocks, counts_hbm, target_hbm, source_hbm, tiles_hbm, grads_hbm, *rest):
    n = len(ranges)
    outs = rest[:n]
    acc, listed, counts, target, source, tiles, grads, sems = rest[n:]
    copies = [
        pltpu.make_async_copy(there, here, sems.at[i])
        for i, (there, here) in enumerate(
            [
                (counts_hbm, counts),
                (source_hbm, source),
                (target_hbm, target),
                (grads_hbm, grads),
                (tiles_hbm, tiles),
            ]
        )
    ]
    for copy in copies:
        copy.start()
    acc[...] = jnp.zeros_like(acc)
    for copy in copies:
        copy.wait()
    for low, out in zip(ranges, outs):
        if low != ranges[0]:
            acc[...] = jnp.zeros_like(acc)
        found = pick(listed, counts[0, 0], source, low, low + nblocks)

        def step(k, valid):
            at = jnp.where(valid, source[0, k] - low, nblocks)
            acc[at] += lax.dot_general(
                tiles[k], grads[target[0, k]], (((0,), (0,)), ((), ())), preferred_element_type=F32
            )

        over_tiles(listed, found, step)
        for b in range(nblocks):
            out[b] = acc[b].astype(out.dtype)


def triplet_body(lows, nblocks, counts, target, source, tiles, *rest):
    n = len(lows)
    rows, start, out, acc, listed = rest[:n], *rest[n:]
    for b in range(nblocks):
        acc[b] = start[b].astype(F32)
    for low, piece in zip(lows, rows):
        found = pick(listed, counts[0, 0], source, low, low + piece.shape[0])

        def step(k, valid):
            at = jnp.where(valid, target[0, k], nblocks)
            s = jnp.where(valid, source[0, k] - low, 0)
            acc[at] += jnp.dot(tiles[k], piece[s], preferred_element_type=F32)

        over_tiles(listed, found, step)
    for b in range(nblocks):
        out[b] = acc[b].astype(out.dtype)


def preact_body(step, mine, theirs, weight, act, factor, flipped):
    rows, chans = mine.shape
    core = lax.axis_index("tensor")
    own = pl.ds(pl.multiple_of(core * chans, chans), chans)
    other = pl.ds(pl.multiple_of((1 - core) * chans, chans), chans)
    for r in range(0, rows, step):
        at = pl.ds(r, step)
        pre = jnp.dot(mine[at], weight[own], preferred_element_type=F32) + jnp.dot(
            theirs[at], weight[other], preferred_element_type=F32
        )
        sig = 1.0 / (1.0 + jnp.exp(-pre))
        act[at] = (pre * sig).astype(BF16)
        factor[at] = sig * (1.0 + pre * (1.0 - sig))
        flipped[own, at] = mine[at].T
        flipped[other, at] = theirs[at].T


def partners():
    return [(f, d) for f in (1, 0) for d in range(lax.axis_size("dp")) if (f, d) != (0, 0)]


def to_partner(value, flip, steps):
    nz, ndp = lax.axis_size("graph"), lax.axis_size("dp")
    pairs = [
        (z * ndp + d, (z ^ flip) * ndp + (d + steps) % ndp) for z in range(nz) for d in range(ndp)
    ]
    return lax.ppermute(value, ("graph", "dp"), pairs)


def place(flip, steps, size):
    ndp = lax.axis_size("dp")
    d = lax.rem(lax.axis_index("dp") + steps + ndp, ndp)
    b = lax.rem(lax.axis_index("graph") + flip, 2)
    return pl.ds(pl.multiple_of((d * 2 + b) * size, size), size)


def slope_body(step, back, from_next, from_prev, factor, grads, weight, flipped, *rest):
    to_core, gsum, keep = rest[:3]
    others = partners()
    sends = rest[3 : 3 + len(others)]
    slope, part = rest[3 + len(others) :]
    rows, chans = grads.shape
    core = lax.axis_index("tensor")
    own = pl.ds(pl.multiple_of(core * chans, chans), chans)
    other = pl.ds(pl.multiple_of((1 - core) * chans, chans), chans)
    last = (((1,), (1,)), ((), ()))
    for r in range(0, rows, step):
        at = pl.ds(r, step)
        total = back[at] + from_next[at].astype(F32) + from_prev[at].astype(F32)
        piece = (total * factor[at]).astype(BF16)
        slope[at] = piece
        to_core[at] = lax.dot_general(piece, weight[other], last, preferred_element_type=F32).astype(BF16)
        gsum[at] = grads[at].astype(F32) + lax.dot_general(
            piece, weight[own], last, preferred_element_type=F32
        )
    part[...] = jnp.dot(flipped[...], slope[...], preferred_element_type=F32)
    size = keep.shape[0]
    keep[...] = part[place(0, 0, size)]
    for (flip, steps), send in zip(others, sends):
        send[...] = part[place(flip, steps, size)].astype(BF16)


def grads_body(gsum, arrived, out):
    out[...] = (gsum[...] + arrived[...].astype(F32)).astype(BF16)


def total_body(scale, *refs):
    total = refs[0][...].astype(F32)
    for ref in refs[1:-1]:
        total = total + ref[...].astype(F32)
    refs[-1][...] = (total * scale).astype(BF16)


def gather_body(mine, *rest):
    out = rest[-1]
    size = mine.shape[0]
    out[place(0, 0, size)] = mine[...].astype(F32)
    for (flip, steps), ref in zip(partners(), rest):
        out[place(flip, -steps, size)] = ref[...].astype(F32)


def bits(nz):
    return [1 << i for i in range(1, nz.bit_length() - 1)]


def shards(edges_in, weight, basis_tiles, target_blocks, source_blocks, counts, grad_out):
    rows, chans = edges_in.shape[1], edges_in.shape[2]
    tile = basis_tiles.shape[2]
    nblocks = rows // tile
    slots = basis_tiles.shape[1]
    depth = weight.shape[0]
    ndp, nz = lax.axis_size("dp"), lax.axis_size("graph")
    mine, grads, tiles = edges_in[0], grad_out[0], basis_tiles[0]
    blocks = (nblocks, tile, chans)
    flat = (rows, chans)
    index = [counts, target_blocks, source_blocks, tiles]
    work = [pltpu.VMEM((nblocks + 1, tile, chans), F32), pltpu.SMEM((slots + UNROLL,), jnp.int32)]
    unit = 2 * tile * tile * chans * slots // 3

    half = nblocks // 2
    theirs = shift(mine, "tensor", 1)

    def back_terms(ranges, kinds):
        return call(
            functools.partial(back_body, ranges, nblocks),
            [*index, grads.reshape(blocks)],
            [(blocks, kind) for kind in kinds],
            work
            + [pltpu.SMEM(x.shape, jnp.int32) for x in index[:3]]
            + [pltpu.VMEM(tiles.shape, BF16), pltpu.VMEM(blocks, BF16), pltpu.SemaphoreType.DMA((5,))],
            flops=len(ranges) * unit,
            nbytes=4 * rows * chans,
            space=HBM,
        )

    to_prev, to_next = back_terms((0, 2 * nblocks), (BF16, BF16))
    from_next = shift(to_prev, "graph", -1)
    from_prev = shift(to_next, "graph", 1)
    (back,) = back_terms((nblocks,), (F32,))
    act, factor, flipped = call(
        functools.partial(preact_body, 256),
        [mine, theirs, weight],
        [(flat, BF16), (flat, F32), ((depth, rows), BF16)],
        flops=2 * rows * depth * chans,
        nbytes=8 * rows * chans,
    )
    act = act.reshape(blocks)
    low_act, high_act = act[:half], act[half:]

    def triplet(lows, pieces, start, kind):
        (acc,) = call(
            functools.partial(triplet_body, lows, nblocks),
            [*index, *pieces, start],
            [(blocks, kind)],
            work,
            flops=unit,
            nbytes=4 * rows * chans,
        )
        return acc

    prev_low = shift(low_act, "graph", 1)
    others = partners()
    size = depth // (len(others) + 1)
    to_core, gsum, keep, *sends = call(
        functools.partial(slope_body, 256),
        [back.reshape(flat), from_next.reshape(flat), from_prev.reshape(flat), factor, grads, weight, flipped],
        [(flat, BF16), (flat, F32), ((size, chans), F32)] + [((size, chans), BF16)] * len(others),
        [pltpu.VMEM(flat, BF16), pltpu.VMEM((depth, chans), F32)],
        flops=4 * rows * depth * chans,
        nbytes=8 * rows * chans,
    )
    arrived = [to_partner(s, *at) for s, at in zip(sends, others)]
    high_now, _ = lax.optimization_barrier((high_act, keep))
    prev_high = shift(high_now, "graph", 1)
    summed = shift(to_core, "tensor", 1)
    (grad_edges,) = call(grads_body, [gsum, summed], [(flat, BF16)], nbytes=8 * rows * chans)

    def add_up(scale, parts):
        return call(functools.partial(total_body, scale), parts, [((size, chans), BF16)])[0]

    scale = float(1.0 / (ndp * edges_in.shape[0] * nz * rows) ** 0.5)
    stages = bits(nz)
    total = add_up(1.0 if stages else scale, [keep, *arrived])
    low_now, _ = lax.optimization_barrier((low_act, total))
    next_low = shift(low_now, "graph", -1)
    for i, bit in enumerate(stages):
        swapped = lax.ppermute(total, "graph", [(z, z ^ bit) for z in range(nz)])
        total = add_up(scale if i + 1 == len(stages) else 1.0, [total, swapped])
    high_now, _ = lax.optimization_barrier((high_act, total))
    next_high = shift(high_now, "graph", -1)
    arrived = [to_partner(total, *at) for at in others]
    (grad_weight,) = call(gather_body, [total, *arrived], [((depth, chans), F32)])

    acc = triplet((nblocks, 0, half), (act, prev_low, prev_high), mine.reshape(blocks), F32)
    acc = triplet((2 * nblocks,), (next_low,), acc, F32)
    edges_out = triplet((2 * nblocks + half,), (next_high,), acc, BF16)
    return edges_out.reshape(1, rows, chans), grad_edges[None], grad_weight


def solution(mesh):
    placed = (
        P(("parts", "dp"), "graph", "tensor"),
        P(None, "tensor"),
        P(("parts", "dp"), "graph", None, None),
        P(("parts", "dp"), "graph"),
        P(("parts", "dp"), "graph"),
        P(("parts", "dp"), "graph"),
        P(("parts", "dp"), "graph", "tensor"),
    )
    return jax.shard_map(
        shards,
        mesh=mesh,
        in_specs=placed,
        out_specs=(
            P(("parts", "dp"), "graph", "tensor"),
            P(("parts", "dp"), "graph", "tensor"),
            P("parts", "tensor"),
        ),
        check_vma=False,
    )
```

```python
import functools

import jax
import jax.numpy as jnp
from jax import lax
from jax.experimental import pallas as pl
from jax.experimental.pallas import tpu as pltpu
from jax.sharding import PartitionSpec as P

F32 = jnp.float32
BF16 = jnp.bfloat16
UNROLL = 4
BACK_COST, PREACT_COST, SLOPE_COST, SUM_COST, GRADS_COST = 1.0, 1.0, 0.5, 0.1, 0.5
TRIPLET_COSTS = (2.0, 1.0, 1.0)
VMEM = pl.BlockSpec(memory_space=pltpu.VMEM)
SMEM = pl.BlockSpec(memory_space=pltpu.SMEM)
HBM = pl.BlockSpec(memory_space=pltpu.HBM)


def call(body, ins, outs, scratch=(), cost=0.0, space=None, limit=32):
    return pl.pallas_call(
        body,
        name=getattr(body, "func", body).__name__,
        in_specs=[space or (SMEM if x.dtype == jnp.int32 else VMEM) for x in ins],
        out_shape=[jax.ShapeDtypeStruct(s, d) for s, d in outs],
        out_specs=[VMEM for _ in outs],
        scratch_shapes=list(scratch),
        cost_estimate=pl.CostEstimate(flops=int(cost * 1.15e9), bytes_accessed=0, transcendentals=0),
        compiler_params=pltpu.CompilerParams(vmem_limit_bytes=limit * 1024 * 1024),
    )(*ins)


def shift(value, axis, steps):
    count = lax.axis_size(axis)
    return lax.ppermute(value, axis, [(i, (i + steps) % count) for i in range(count)])


def after(value, *others):
    return lax.optimization_barrier((value, *others))[0]


def pick(listed, count, source, low, high):
    slots = source.shape[1]

    def step(k, found):
        listed[found] = k
        s = source[0, k]
        inside = (k < count) & (s >= low) & (s < high)
        return found + inside.astype(jnp.int32)

    found = lax.fori_loop(0, slots, step, jnp.int32(0))
    for j in range(UNROLL):
        listed[found + j] = 0
    return found


def over_tiles(listed, found, step):
    def some(i, carry):
        for j in range(UNROLL):
            at = i * UNROLL + j
            step(listed[at], at < found)
        return carry

    lax.fori_loop(0, (found + UNROLL - 1) // UNROLL, some, 0)


def back_body(ranges, nblocks, counts_hbm, target_hbm, source_hbm, tiles_hbm, grads_hbm, *rest):
    n = len(ranges)
    outs = rest[:n]
    acc, listed, counts, target, source, tiles, grads, sems = rest[n:]
    copies = [
        pltpu.make_async_copy(there, here, sems.at[i])
        for i, (there, here) in enumerate(
            [
                (counts_hbm, counts),
                (source_hbm, source),
                (target_hbm, target),
                (grads_hbm, grads),
                (tiles_hbm, tiles),
            ]
        )
    ]
    for copy in copies:
        copy.start()
    acc[...] = jnp.zeros_like(acc)
    for copy in copies:
        copy.wait()
    for low, out in zip(ranges, outs):
        if low != ranges[0]:
            acc[...] = jnp.zeros_like(acc)
        found = pick(listed, counts[0, 0], source, low, low + nblocks)

        def step(k, valid):
            at = jnp.where(valid, source[0, k] - low, nblocks)
            acc[at] += lax.dot_general(
                tiles[k], grads[target[0, k]], (((0,), (0,)), ((), ())), preferred_element_type=F32
            )

        over_tiles(listed, found, step)
        for b in range(nblocks):
            out[b] = acc[b].astype(out.dtype)


def triplet_body(lows, nblocks, counts, target, source, tiles, *rest):
    n = len(lows)
    rows, start, out, acc, listed = rest[:n], *rest[n:]
    for b in range(nblocks):
        acc[b] = start[b].astype(F32)
    for low, piece in zip(lows, rows):
        found = pick(listed, counts[0, 0], source, low, low + piece.shape[0])

        def step(k, valid):
            at = jnp.where(valid, target[0, k], nblocks)
            s = jnp.where(valid, source[0, k] - low, 0)
            acc[at] += jnp.dot(tiles[k], piece[s], preferred_element_type=F32)

        over_tiles(listed, found, step)
    for b in range(nblocks):
        out[b] = acc[b].astype(out.dtype)


def preact_body(step, mine, theirs, weight, low_act, high_act, factor, flipped):
    rows, chans = mine.shape
    core = lax.axis_index("tensor")
    own = pl.ds(pl.multiple_of(core * chans, chans), chans)
    other = pl.ds(pl.multiple_of((1 - core) * chans, chans), chans)
    for r in range(0, rows, step):
        at = pl.ds(r, step)
        pre = jnp.dot(mine[at], weight[own], preferred_element_type=F32) + jnp.dot(
            theirs[at], weight[other], preferred_element_type=F32
        )
        sig = 1.0 / (1.0 + jnp.exp(-pre))
        act, inside = (low_act, r) if r < rows // 2 else (high_act, r - rows // 2)
        act[pl.ds(inside, step)] = (pre * sig).astype(BF16)
        factor[at] = sig * (1.0 + pre * (1.0 - sig))
        flipped[own, at] = mine[at].T
        flipped[other, at] = theirs[at].T


def activate_body(mine, theirs, weight, act):
    chans = mine.shape[1]
    core = lax.axis_index("tensor")
    own = pl.ds(pl.multiple_of(core * chans, chans), chans)
    other = pl.ds(pl.multiple_of((1 - core) * chans, chans), chans)
    pre = jnp.dot(mine[...], weight[own], preferred_element_type=F32) + jnp.dot(
        theirs[...], weight[other], preferred_element_type=F32
    )
    act[...] = (pre / (1.0 + jnp.exp(-pre))).astype(BF16)


def partners():
    return [(f, d) for f in (1, 0) for d in range(lax.axis_size("dp")) if (f, d) != (0, 0)]


def to_partner(value, flip, steps):
    nz, ndp = lax.axis_size("graph"), lax.axis_size("dp")
    pairs = [
        (z * ndp + d, (z ^ flip) * ndp + (d + steps) % ndp) for z in range(nz) for d in range(ndp)
    ]
    return lax.ppermute(value, ("graph", "dp"), pairs)


def place(flip, steps, size):
    ndp = lax.axis_size("dp")
    d = lax.rem(lax.axis_index("dp") + steps + ndp, ndp)
    b = lax.rem(lax.axis_index("graph") + flip, 2)
    return pl.ds(pl.multiple_of((d * 2 + b) * size, size), size)


def slope_body(step, back, from_next, from_prev, factor, grads, weight, flipped, *rest):
    to_core, gsum, keep = rest[:3]
    others = partners()
    sends = rest[3 : 3 + len(others)]
    slope, part = rest[3 + len(others) :]
    rows, chans = grads.shape
    core = lax.axis_index("tensor")
    own = pl.ds(pl.multiple_of(core * chans, chans), chans)
    other = pl.ds(pl.multiple_of((1 - core) * chans, chans), chans)
    last = (((1,), (1,)), ((), ()))
    for r in range(0, rows, step):
        at = pl.ds(r, step)
        total = back[at] + from_next[at].astype(F32) + from_prev[at].astype(F32)
        piece = (total * factor[at]).astype(BF16)
        slope[at] = piece
        to_core[at] = lax.dot_general(piece, weight[other], last, preferred_element_type=F32).astype(BF16)
        gsum[at] = grads[at].astype(F32) + lax.dot_general(
            piece, weight[own], last, preferred_element_type=F32
        )
    part[...] = jnp.dot(flipped[...], slope[...], preferred_element_type=F32)
    size = keep.shape[0]
    keep[...] = part[place(0, 0, size)]
    for (flip, steps), send in zip(others, sends):
        send[...] = part[place(flip, steps, size)].astype(BF16)


def grads_body(gsum, arrived, out):
    out[...] = (gsum[...] + arrived[...].astype(F32)).astype(BF16)


def total_body(scale, *refs):
    total = refs[0][...].astype(F32)
    for ref in refs[1:-1]:
        total = total + ref[...].astype(F32)
    refs[-1][...] = (total * scale).astype(BF16)


def gather_body(mine, *rest):
    out = rest[-1]
    size = mine.shape[0]
    out[place(0, 0, size)] = mine[...].astype(F32)
    for (flip, steps), ref in zip(partners(), rest):
        out[place(flip, -steps, size)] = ref[...].astype(F32)


def bits(nz):
    return [1 << i for i in range(1, nz.bit_length() - 1)]


def shards(edges_in, weight, basis_tiles, target_blocks, source_blocks, counts, grad_out):
    rows, chans = edges_in.shape[1], edges_in.shape[2]
    tile = basis_tiles.shape[2]
    nblocks = rows // tile
    slots = basis_tiles.shape[1]
    depth = weight.shape[0]
    ndp, nz = lax.axis_size("dp"), lax.axis_size("graph")
    mine, grads, tiles = edges_in[0], grad_out[0], basis_tiles[0]
    blocks = (nblocks, tile, chans)
    flat = (rows, chans)
    index = [counts, target_blocks, source_blocks, tiles]
    work = [pltpu.VMEM((nblocks + 1, tile, chans), F32), pltpu.SMEM((slots + UNROLL,), jnp.int32)]

    half = nblocks // 2
    quarter = (half, tile, chans)
    theirs = shift(mine, "tensor", 1)
    prev_rows = shift(mine[: rows // 2], "graph", 1)

    def back_terms(ranges, kinds):
        return call(
            functools.partial(back_body, ranges, nblocks),
            [*index, grads.reshape(blocks)],
            [(blocks, kind) for kind in kinds],
            work
            + [pltpu.SMEM(x.shape, jnp.int32) for x in index[:3]]
            + [pltpu.VMEM(tiles.shape, BF16), pltpu.VMEM(blocks, BF16), pltpu.SemaphoreType.DMA((5,))],
            cost=BACK_COST,
            space=HBM,
            limit=58,
        )

    (to_prev,) = back_terms((0,), (BF16,))
    from_next = shift(to_prev, "graph", -1)
    to_next, back = back_terms((2 * nblocks, nblocks), (BF16, F32))
    from_prev = shift(to_next, "graph", 1)
    low_act, high_act, factor, flipped = call(
        functools.partial(preact_body, 256),
        [mine, theirs, weight],
        [((rows // 2, chans), BF16)] * 2 + [(flat, F32), ((depth, rows), BF16)],
        cost=PREACT_COST,
    )
    low_act = low_act.reshape(quarter)
    high_act = high_act.reshape(quarter)
    prev_high = shift(high_act, "graph", 1)
    (prev_low,) = call(
        activate_body,
        [prev_rows, shift(prev_rows, "tensor", 1), weight],
        [((rows // 2, chans), BF16)],
        cost=PREACT_COST,
    )
    prev_low = prev_low.reshape(quarter)

    others = partners()
    size = depth // (len(others) + 1)
    to_core, gsum, keep, *sends = call(
        functools.partial(slope_body, 256),
        [after(back, prev_low).reshape(flat), from_next.reshape(flat), from_prev.reshape(flat), factor, grads, weight, flipped],
        [(flat, BF16), (flat, F32), ((size, chans), F32)] + [((size, chans), BF16)] * len(others),
        [pltpu.VMEM(flat, BF16), pltpu.VMEM((depth, chans), F32)],
        cost=SLOPE_COST,
    )
    arrived = [to_partner(s, *at) for s, at in zip(sends, others)]
    next_low = shift(after(low_act, keep), "graph", -1)
    summed = shift(to_core, "tensor", 1)
    (grad_edges,) = call(grads_body, [gsum, summed], [(flat, BF16)], cost=GRADS_COST)

    def triplet(lows, pieces, start, kind, cost):
        (acc,) = call(
            functools.partial(triplet_body, lows, nblocks),
            [*index, *pieces, start],
            [(blocks, kind)],
            work,
            cost=cost,
        )
        return acc

    def add_up(scale, parts):
        return call(functools.partial(total_body, scale), parts, [((size, chans), BF16)], cost=SUM_COST)[0]

    scale = float(1.0 / (ndp * edges_in.shape[0] * nz * rows) ** 0.5)
    stages = bits(nz)
    total = add_up(1.0 if stages else scale, [after(keep, prev_high), *arrived])
    next_high = shift(after(high_act, total), "graph", -1)
    acc = triplet(
        (nblocks, nblocks + half, 0, half),
        (low_act, high_act, prev_low, prev_high),
        mine.reshape(blocks),
        F32,
        TRIPLET_COSTS[0],
    )
    for i, bit in enumerate(stages):
        swapped = lax.ppermute(total, "graph", [(z, z ^ bit) for z in range(nz)])
        total = add_up(scale if i + 1 == len(stages) else 1.0, [after(total, next_low, acc, grad_edges), swapped])
    acc = triplet((2 * nblocks,), (next_low,), acc, F32, TRIPLET_COSTS[1])
    arrived = [to_partner(total, *at) for at in others]
    (grad_weight,) = call(gather_body, [after(total, next_high, acc), *arrived], [((depth, chans), F32)], cost=SUM_COST)

    edges_out = triplet((2 * nblocks + half,), (next_high,), acc, BF16, TRIPLET_COSTS[2])
    return edges_out.reshape(1, rows, chans), grad_edges[None], grad_weight


def solution(mesh):
    placed = (
        P(("parts", "dp"), "graph", "tensor"),
        P(None, "tensor"),
        P(("parts", "dp"), "graph", None, None),
        P(("parts", "dp"), "graph"),
        P(("parts", "dp"), "graph"),
        P(("parts", "dp"), "graph"),
        P(("parts", "dp"), "graph", "tensor"),
    )
    return jax.shard_map(
        shards,
        mesh=mesh,
        in_specs=placed,
        out_specs=(
            P(("parts", "dp"), "graph", "tensor"),
            P(("parts", "dp"), "graph", "tensor"),
            P("parts", "tensor"),
        ),
        check_vma=False,
    )
```

```python
import functools

import jax
import jax.numpy as jnp
from jax import lax
from jax.experimental import pallas as pl
from jax.experimental.pallas import tpu as pltpu
from jax.sharding import PartitionSpec as P

F32 = jnp.float32
BF16 = jnp.bfloat16
UNROLL = 4
LEAD = 5
FIRST = 4
BACK_COST, PREACT_COST, SLOPE_COST, SUM_COST, GATHER_COST, GRADS_COST = 1.0, 1.0, 0.5, 2.0, 3.0, 0.5
TICK_COSTS = (3.0, 0.3)
TRIPLET_COSTS = (0.5, 0.3, 0.3, 6.0)
VMEM = pl.BlockSpec(memory_space=pltpu.VMEM)
SMEM = pl.BlockSpec(memory_space=pltpu.SMEM)
HBM = pl.BlockSpec(memory_space=pltpu.HBM)
ANY = pl.BlockSpec(memory_space=pl.ANY)


def call(body, ins, outs, scratch=(), cost=0.0, space=None, limit=32, waits=(), carried=()):
    n, extra = len(ins), len(waits) + len(carried)

    def kernel(*refs):
        results = refs[n + extra :]
        body(*refs[:n], *results[: len(outs)], *results[len(outs) + len(carried) :])

    return pl.pallas_call(
        kernel,
        name=getattr(body, "func", body).__name__,
        in_specs=[space or (SMEM if x.dtype == jnp.int32 else VMEM) for x in ins] + [ANY] * extra,
        out_shape=[jax.ShapeDtypeStruct(s, d) for s, d in outs]
        + [jax.ShapeDtypeStruct(x.shape, x.dtype) for x in carried],
        out_specs=[VMEM for _ in outs] + [ANY for _ in carried],
        scratch_shapes=list(scratch),
        input_output_aliases={n + len(waits) + i: len(outs) + i for i in range(len(carried))},
        cost_estimate=pl.CostEstimate(flops=int(cost * 1.15e9), bytes_accessed=0, transcendentals=0),
        compiler_params=pltpu.CompilerParams(vmem_limit_bytes=limit * 1024 * 1024),
    )(*ins, *waits, *carried)


def shift(value, axis, steps):
    count = lax.axis_size(axis)
    return lax.ppermute(value, axis, [(i, (i + steps) % count) for i in range(count)])


def pick(listed, count, source, low, high):
    slots = source.shape[1]

    found = jnp.int32(0)
    for k in range(slots):
        listed[found] = k
        s = source[0, k]
        inside = (k < count) & (s >= low) & (s < high)
        found = found + inside.astype(jnp.int32)
    for j in range(UNROLL):
        listed[found + j] = 0
    return found


def over_tiles(listed, found, step):
    def some(i, carry):
        for j in range(UNROLL):
            at = i * UNROLL + j
            step(listed[at], at < found)
        return carry

    lax.fori_loop(0, (found + UNROLL - 1) // UNROLL, some, 0)


def back_body(ranges, nblocks, counts_hbm, target_hbm, source_hbm, tiles_hbm, grads_hbm, *rest):
    n = len(ranges)
    outs = rest[:n]
    acc, listed, counts, target, source, tiles, grads, sems = rest[n:]
    copies = [
        pltpu.make_async_copy(there, here, sems.at[i])
        for i, (there, here) in enumerate(
            [
                (counts_hbm, counts),
                (source_hbm, source),
                (target_hbm, target),
                (grads_hbm, grads),
                (tiles_hbm, tiles),
            ]
        )
    ]
    for copy in copies:
        copy.start()
    acc[...] = jnp.zeros_like(acc)
    for copy in copies[:3]:
        copy.wait()
    for low, out in zip(ranges, outs):
        if low != ranges[0]:
            acc[...] = jnp.zeros_like(acc)
        found = pick(listed, counts[0, 0], source, low, low + nblocks)
        if low == ranges[0]:
            for copy in copies[3:]:
                copy.wait()

        def step(k, valid):
            at = jnp.where(valid, source[0, k] - low, nblocks)
            acc[at] += lax.dot_general(
                tiles[k], grads[target[0, k]], (((0,), (0,)), ((), ())), preferred_element_type=F32
            )

        over_tiles(listed, found, step)
        for b in range(nblocks):
            out[b] = acc[b].astype(out.dtype)


def triplet_body(lows, nblocks, counts, target, source, tiles, *rest):
    n = len(lows)
    rows, start, out, acc, listed = rest[:n], *rest[n:]
    for b in range(nblocks):
        acc[b] = start[b].astype(F32)
    for low, piece in zip(lows, rows):
        found = pick(listed, counts[0, 0], source, low, low + piece.shape[0])

        def step(k, valid):
            at = jnp.where(valid, target[0, k], nblocks)
            s = jnp.where(valid, source[0, k] - low, 0)
            acc[at] += jnp.dot(tiles[k], piece[s], preferred_element_type=F32)

        over_tiles(listed, found, step)
    for b in range(nblocks):
        out[b] = acc[b].astype(out.dtype)


def preact_body(step, mine, theirs, weight, act, factor, flipped, up, *down):
    rows, chans = mine.shape
    core = lax.axis_index("tensor")
    own = pl.ds(pl.multiple_of(core * chans, chans), chans)
    other = pl.ds(pl.multiple_of((1 - core) * chans, chans), chans)
    for r in range(0, rows, step):
        at = pl.ds(r, step)
        pre = jnp.dot(mine[at], weight[own], preferred_element_type=F32) + jnp.dot(
            theirs[at], weight[other], preferred_element_type=F32
        )
        sig = 1.0 / (1.0 + jnp.exp(-pre))
        act[at] = (pre * sig).astype(BF16)
        factor[at] = sig * (1.0 + pre * (1.0 - sig))
        flipped[own, at] = mine[at].T
        flipped[other, at] = theirs[at].T
    up[...] = act[pl.ds(rows - up.shape[0], up.shape[0])]
    begin = 0
    for piece in down:
        piece[...] = act[pl.ds(begin, piece.shape[0])]
        begin += piece.shape[0]


def tick_body(out):
    out[...] = jnp.zeros_like(out)


def activate_body(mine, theirs, weight, act):
    chans = mine.shape[1]
    core = lax.axis_index("tensor")
    own = pl.ds(pl.multiple_of(core * chans, chans), chans)
    other = pl.ds(pl.multiple_of((1 - core) * chans, chans), chans)
    pre = jnp.dot(mine[...], weight[own], preferred_element_type=F32) + jnp.dot(
        theirs[...], weight[other], preferred_element_type=F32
    )
    act[...] = (pre / (1.0 + jnp.exp(-pre))).astype(BF16)


def partners():
    return [(f, d) for f in (1, 0) for d in range(lax.axis_size("dp")) if (f, d) != (0, 0)]


def to_partner(value, flip, steps):
    nz, ndp = lax.axis_size("graph"), lax.axis_size("dp")
    pairs = [
        (z * ndp + d, (z ^ flip) * ndp + (d + steps) % ndp) for z in range(nz) for d in range(ndp)
    ]
    return lax.ppermute(value, ("graph", "dp"), pairs)


def swap(value, bit):
    return lax.ppermute(value, "graph", [(z, z ^ bit) for z in range(lax.axis_size("graph"))])


def place(flip, steps, size):
    ndp = lax.axis_size("dp")
    d = lax.rem(lax.axis_index("dp") + steps + ndp, ndp)
    b = lax.rem(lax.axis_index("graph") + flip, 2)
    return pl.ds(pl.multiple_of((d * 2 + b) * size, size), size)


def slope_body(step, back, from_next, from_prev, factor, grads, weight, flipped, *rest):
    to_core, gsum, keep = rest[:3]
    others = partners()
    sends = rest[3 : 3 + len(others)]
    slope, part = rest[3 + len(others) :]
    rows, chans = grads.shape
    core = lax.axis_index("tensor")
    own = pl.ds(pl.multiple_of(core * chans, chans), chans)
    other = pl.ds(pl.multiple_of((1 - core) * chans, chans), chans)
    last = (((1,), (1,)), ((), ()))
    for r in range(0, rows, step):
        at = pl.ds(r, step)
        total = back[at] + from_next[at].astype(F32) + from_prev[at].astype(F32)
        piece = (total * factor[at]).astype(BF16)
        slope[at] = piece
        to_core[at] = lax.dot_general(piece, weight[other], last, preferred_element_type=F32).astype(BF16)
        gsum[at] = grads[at].astype(F32) + lax.dot_general(
            piece, weight[own], last, preferred_element_type=F32
        )
    part[...] = jnp.dot(flipped[...], slope[...], preferred_element_type=F32)
    size = keep.shape[0]
    keep[...] = part[place(0, 0, size)]
    for (flip, steps), send in zip(others, sends):
        send[...] = part[place(flip, steps, size)].astype(BF16)


def grads_body(gsum, arrived, out, token):
    token[...] = jnp.zeros_like(token)
    out[...] = (gsum[...] + arrived[...].astype(F32)).astype(BF16)


def total_body(scale, *refs):
    total = refs[0][...].astype(F32)
    for ref in refs[1:-1]:
        total = total + ref[...].astype(F32)
    refs[-1][...] = (total * scale).astype(BF16)


def gather_body(mine, *rest):
    out = rest[-1]
    size = mine.shape[0]
    out[place(0, 0, size)] = mine[...].astype(F32)
    for (flip, steps), ref in zip(partners(), rest):
        out[place(flip, -steps, size)] = ref[...].astype(F32)


def bits(nz):
    return [1 << i for i in range(1, nz.bit_length() - 1)]


def shards(edges_in, weight, basis_tiles, target_blocks, source_blocks, counts, grad_out):
    rows, chans = edges_in.shape[1], edges_in.shape[2]
    tile = basis_tiles.shape[2]
    nblocks = rows // tile
    slots = basis_tiles.shape[1]
    depth = weight.shape[0]
    ndp, nz = lax.axis_size("dp"), lax.axis_size("graph")
    mine, grads, tiles = edges_in[0], grad_out[0], basis_tiles[0]
    blocks = (nblocks, tile, chans)
    flat = (rows, chans)
    index = [counts, target_blocks, source_blocks, tiles]
    work = [pltpu.VMEM((nblocks + 1, tile, chans), F32), pltpu.SMEM((slots + UNROLL,), jnp.int32)]

    theirs = shift(mine, "tensor", 1)
    lead = min(LEAD, nblocks - 1)
    prev_rows = shift(mine[: lead * tile], "graph", 1)

    def back_terms(ranges, kinds, waits=()):
        return call(
            functools.partial(back_body, ranges, nblocks),
            [*index, grads.reshape(blocks)],
            [(blocks, kind) for kind in kinds],
            work
            + [pltpu.SMEM(x.shape, jnp.int32) for x in index[:3]]
            + [pltpu.VMEM(tiles.shape, BF16), pltpu.VMEM(blocks, BF16), pltpu.SemaphoreType.DMA((5,))],
            cost=BACK_COST,
            space=HBM,
            limit=58,
            waits=waits,
        )

    def tick(cost, *waits):
        return call(tick_body, [], [((8, 128), F32)], cost=cost, waits=waits)[0]

    def triplet(lows, pieces, start, kind, cost):
        return call(
            functools.partial(triplet_body, lows, nblocks),
            [*index, *pieces, start],
            [(blocks, kind)],
            work,
            cost=cost,
        )[0]

    (to_prev,) = back_terms((0,), (BF16,))
    from_next = shift(to_prev, "graph", -1)
    to_next, back = back_terms((2 * nblocks, nblocks), (BF16, F32), [to_prev])
    from_prev = shift(to_next, "graph", 1)
    cuts = [0, min(FIRST, nblocks - 1), nblocks]
    sizes = [nblocks - lead] + [high - low for low, high in zip(cuts, cuts[1:])]
    act, factor, flipped, *sent = call(
        functools.partial(preact_body, 256),
        [mine, theirs, weight],
        [(flat, BF16), (flat, F32), ((depth, rows), BF16)] + [((n * tile, chans), BF16) for n in sizes],
        cost=PREACT_COST,
    )
    up, first, second = [x.reshape(-1, tile, chans) for x in sent]
    prev_high = shift(up, "graph", 1)
    (prev_low,) = call(
        activate_body,
        [prev_rows, shift(prev_rows, "tensor", 1), weight],
        [((lead * tile, chans), BF16)],
        cost=PREACT_COST,
    )
    prev_low = prev_low.reshape(lead, tile, chans)
    others = partners()
    size = depth // (len(others) + 1)
    part = ((size, chans), BF16)
    to_core, gsum, keep, *sends, first = call(
        functools.partial(slope_body, 256),
        [back.reshape(flat), from_next.reshape(flat), from_prev.reshape(flat), factor, grads, weight, flipped],
        [(flat, BF16), (flat, F32), ((size, chans), F32)] + [part] * len(others),
        [pltpu.VMEM(flat, BF16), pltpu.VMEM((depth, chans), F32)],
        cost=SLOPE_COST,
        waits=[prev_low],
        carried=[first],
    )
    arrived = [to_partner(s, *at) for s, at in zip(sends, others)]
    next_first = shift(first, "graph", -1)
    summed = shift(to_core, "tensor", 1)
    grad_edges, token = call(grads_body, [gsum, summed], [(flat, BF16), ((8, 128), F32)], cost=GRADS_COST)
    acc = triplet((0, nblocks), (prev_low, act.reshape(blocks)), mine.reshape(blocks), F32, TRIPLET_COSTS[0])
    scale = float(1.0 / (ndp * edges_in.shape[0] * nz * rows) ** 0.5)
    stages = bits(nz)
    total, second = call(
        functools.partial(total_body, 1.0 if stages else scale),
        [keep, *arrived],
        [part],
        cost=SUM_COST,
        waits=[acc, tick(TICK_COSTS[0], prev_high)],
        carried=[second],
    )
    next_second = shift(second, "graph", -1)
    acc = triplet((lead,), (prev_high,), acc, F32, TRIPLET_COSTS[1])
    waits = [token, acc, tick(TICK_COSTS[1], next_first)]
    for bit in stages:
        (total,) = call(
            functools.partial(total_body, scale if bit == stages[-1] else 1.0),
            [total, swap(total, bit)],
            [part],
            cost=SUM_COST,
            waits=waits,
        )
    arrived = [to_partner(total, *at) for at in others]
    acc = triplet((2 * nblocks,), (next_first,), acc, F32, TRIPLET_COSTS[2])
    (grad_weight,) = call(
        gather_body,
        [total, *arrived],
        [((depth, chans), F32)],
        cost=GATHER_COST,
    )
    edges_out = triplet((2 * nblocks + cuts[1],), (next_second,), acc, BF16, TRIPLET_COSTS[3])
    return edges_out.reshape(1, rows, chans), grad_edges[None], grad_weight


def solution(mesh):
    placed = (
        P(("parts", "dp"), "graph", "tensor"),
        P(None, "tensor"),
        P(("parts", "dp"), "graph", None, None),
        P(("parts", "dp"), "graph"),
        P(("parts", "dp"), "graph"),
        P(("parts", "dp"), "graph"),
        P(("parts", "dp"), "graph", "tensor"),
    )
    return jax.shard_map(
        shards,
        mesh=mesh,
        in_specs=placed,
        out_specs=(
            P(("parts", "dp"), "graph", "tensor"),
            P(("parts", "dp"), "graph", "tensor"),
            P("parts", "tensor"),
        ),
        check_vma=False,
    )
```

```python
import functools

import jax
import jax.numpy as jnp
from jax import lax
from jax.experimental import pallas as pl
from jax.experimental.pallas import tpu as pltpu
from jax.sharding import PartitionSpec as P

F32 = jnp.float32
BF16 = jnp.bfloat16
UNROLL = 4
LEAD = 4
FIRST = 4
BACK_COST, PREACT_COST, SLOPE_COST, SUM_COST, GATHER_COST, GRADS_COST = 1.0, 1.0, 0.5, 2.0, 3.0, 0.5
TICK_COSTS = (3.0, 0.3)
TRIPLET_COSTS = (0.5, 0.3, 0.3, 6.0)
VMEM = pl.BlockSpec(memory_space=pltpu.VMEM)
SMEM = pl.BlockSpec(memory_space=pltpu.SMEM)
HBM = pl.BlockSpec(memory_space=pltpu.HBM)
ANY = pl.BlockSpec(memory_space=pl.ANY)


def call(body, ins, outs, scratch=(), cost=0.0, space=None, limit=32, waits=(), carried=()):
    n, extra = len(ins), len(waits) + len(carried)

    def kernel(*refs):
        results = refs[n + extra :]
        body(*refs[:n], *results[: len(outs)], *results[len(outs) + len(carried) :])

    return pl.pallas_call(
        kernel,
        name=getattr(body, "func", body).__name__,
        in_specs=[space or (SMEM if x.dtype == jnp.int32 else VMEM) for x in ins] + [ANY] * extra,
        out_shape=[jax.ShapeDtypeStruct(s, d) for s, d in outs]
        + [jax.ShapeDtypeStruct(x.shape, x.dtype) for x in carried],
        out_specs=[VMEM for _ in outs] + [ANY for _ in carried],
        scratch_shapes=list(scratch),
        input_output_aliases={n + len(waits) + i: len(outs) + i for i in range(len(carried))},
        cost_estimate=pl.CostEstimate(flops=int(cost * 1.15e9), bytes_accessed=0, transcendentals=0),
        compiler_params=pltpu.CompilerParams(vmem_limit_bytes=limit * 1024 * 1024),
    )(*ins, *waits, *carried)


def shift(value, axis, steps):
    count = lax.axis_size(axis)
    return lax.ppermute(value, axis, [(i, (i + steps) % count) for i in range(count)])


def pick(listed, count, source, low, high):
    slots = source.shape[1]

    found = jnp.int32(0)
    for k in range(slots):
        listed[found] = k
        s = source[0, k]
        inside = (k < count) & (s >= low) & (s < high)
        found = found + inside.astype(jnp.int32)
    for j in range(UNROLL):
        listed[found + j] = 0
    return found


def over_tiles(listed, found, step):
    def some(i, carry):
        for j in range(UNROLL):
            at = i * UNROLL + j
            step(listed[at], at < found)
        return carry

    lax.fori_loop(0, (found + UNROLL - 1) // UNROLL, some, 0)


def back_body(ranges, nblocks, counts_hbm, target_hbm, source_hbm, tiles_hbm, grads_hbm, *rest):
    n = len(ranges)
    outs = rest[:n]
    acc, listed, counts, target, source, tiles, grads, sems = rest[n:]
    copies = [
        pltpu.make_async_copy(there, here, sems.at[i])
        for i, (there, here) in enumerate(
            [
                (counts_hbm, counts),
                (source_hbm, source),
                (target_hbm, target),
                (grads_hbm, grads),
                (tiles_hbm, tiles),
            ]
        )
    ]
    for copy in copies:
        copy.start()
    acc[...] = jnp.zeros_like(acc)
    for copy in copies[:3]:
        copy.wait()
    for low, out in zip(ranges, outs):
        if low != ranges[0]:
            acc[...] = jnp.zeros_like(acc)
        found = pick(listed, counts[0, 0], source, low, low + nblocks)
        if low == ranges[0]:
            for copy in copies[3:]:
                copy.wait()

        def step(k, valid):
            at = jnp.where(valid, source[0, k] - low, nblocks)
            acc[at] += lax.dot_general(
                tiles[k], grads[target[0, k]], (((0,), (0,)), ((), ())), preferred_element_type=F32
            )

        over_tiles(listed, found, step)
        for b in range(nblocks):
            out[b] = acc[b].astype(out.dtype)


def triplet_body(lows, nblocks, counts, target, source, tiles, *rest):
    n = len(lows)
    rows, start, out, acc, listed = rest[:n], *rest[n:]
    for b in range(nblocks):
        acc[b] = start[b].astype(F32)
    for low, piece in zip(lows, rows):
        found = pick(listed, counts[0, 0], source, low, low + piece.shape[0])

        def step(k, valid):
            at = jnp.where(valid, target[0, k], nblocks)
            s = jnp.where(valid, source[0, k] - low, 0)
            acc[at] += jnp.dot(tiles[k], piece[s], preferred_element_type=F32)

        over_tiles(listed, found, step)
    for b in range(nblocks):
        out[b] = acc[b].astype(out.dtype)


def preact_body(step, mine, theirs, weight, act, factor, flipped, up, *down):
    rows, chans = mine.shape
    core = lax.axis_index("tensor")
    own = pl.ds(pl.multiple_of(core * chans, chans), chans)
    other = pl.ds(pl.multiple_of((1 - core) * chans, chans), chans)
    for r in range(0, rows, step):
        at = pl.ds(r, step)
        pre = jnp.dot(mine[at], weight[own], preferred_element_type=F32) + jnp.dot(
            theirs[at], weight[other], preferred_element_type=F32
        )
        sig = 1.0 / (1.0 + jnp.exp(-pre))
        act[at] = (pre * sig).astype(BF16)
        factor[at] = sig * (1.0 + pre * (1.0 - sig))
        flipped[own, at] = mine[at].T
        flipped[other, at] = theirs[at].T
    up[...] = act[pl.ds(rows - up.shape[0], up.shape[0])]
    begin = 0
    for piece in down:
        piece[...] = act[pl.ds(begin, piece.shape[0])]
        begin += piece.shape[0]


def tick_body(out):
    out[...] = jnp.zeros_like(out)


def activate_body(mine, theirs, weight, act):
    chans = mine.shape[1]
    core = lax.axis_index("tensor")
    own = pl.ds(pl.multiple_of(core * chans, chans), chans)
    other = pl.ds(pl.multiple_of((1 - core) * chans, chans), chans)
    pre = jnp.dot(mine[...], weight[own], preferred_element_type=F32) + jnp.dot(
        theirs[...], weight[other], preferred_element_type=F32
    )
    act[...] = (pre / (1.0 + jnp.exp(-pre))).astype(BF16)


def partners():
    return [(f, d) for f in (1, 0) for d in range(lax.axis_size("dp")) if (f, d) != (0, 0)]


def to_partner(value, flip, steps):
    nz, ndp = lax.axis_size("graph"), lax.axis_size("dp")
    pairs = [
        (z * ndp + d, (z ^ flip) * ndp + (d + steps) % ndp) for z in range(nz) for d in range(ndp)
    ]
    return lax.ppermute(value, ("graph", "dp"), pairs)


def swap(value, bit):
    return lax.ppermute(value, "graph", [(z, z ^ bit) for z in range(lax.axis_size("graph"))])


def place(flip, steps, size):
    ndp = lax.axis_size("dp")
    d = lax.rem(lax.axis_index("dp") + steps + ndp, ndp)
    b = lax.rem(lax.axis_index("graph") + flip, 2)
    return pl.ds(pl.multiple_of((d * 2 + b) * size, size), size)


def slope_body(step, back, from_next, from_prev, factor, grads, weight, flipped, *rest):
    to_core, gsum, keep = rest[:3]
    others = partners()
    sends = rest[3 : 3 + len(others)]
    slope, part = rest[3 + len(others) :]
    rows, chans = grads.shape
    core = lax.axis_index("tensor")
    own = pl.ds(pl.multiple_of(core * chans, chans), chans)
    other = pl.ds(pl.multiple_of((1 - core) * chans, chans), chans)
    last = (((1,), (1,)), ((), ()))
    for r in range(0, rows, step):
        at = pl.ds(r, step)
        total = back[at] + from_next[at].astype(F32) + from_prev[at].astype(F32)
        piece = (total * factor[at]).astype(BF16)
        slope[at] = piece
        to_core[at] = lax.dot_general(piece, weight[other], last, preferred_element_type=F32).astype(BF16)
        gsum[at] = grads[at].astype(F32) + lax.dot_general(
            piece, weight[own], last, preferred_element_type=F32
        )
    part[...] = jnp.dot(flipped[...], slope[...], preferred_element_type=F32)
    size = keep.shape[0]
    keep[...] = part[place(0, 0, size)]
    for (flip, steps), send in zip(others, sends):
        send[...] = part[place(flip, steps, size)].astype(BF16)


def grads_body(gsum, arrived, out, token):
    token[...] = jnp.zeros_like(token)
    out[...] = (gsum[...] + arrived[...].astype(F32)).astype(BF16)


def total_body(scale, *refs):
    total = refs[0][...].astype(F32)
    for ref in refs[1:-1]:
        total = total + ref[...].astype(F32)
    refs[-1][...] = (total * scale).astype(BF16)


def gather_body(mine, *rest):
    out = rest[-1]
    size = mine.shape[0]
    out[place(0, 0, size)] = mine[...].astype(F32)
    for (flip, steps), ref in zip(partners(), rest):
        out[place(flip, -steps, size)] = ref[...].astype(F32)


def bits(nz):
    return [1 << i for i in range(1, nz.bit_length() - 1)]


def shards(edges_in, weight, basis_tiles, target_blocks, source_blocks, counts, grad_out):
    rows, chans = edges_in.shape[1], edges_in.shape[2]
    tile = basis_tiles.shape[2]
    nblocks = rows // tile
    slots = basis_tiles.shape[1]
    depth = weight.shape[0]
    ndp, nz = lax.axis_size("dp"), lax.axis_size("graph")
    mine, grads, tiles = edges_in[0], grad_out[0], basis_tiles[0]
    blocks = (nblocks, tile, chans)
    flat = (rows, chans)
    index = [counts, target_blocks, source_blocks, tiles]
    work = [pltpu.VMEM((nblocks + 1, tile, chans), F32), pltpu.SMEM((slots + UNROLL,), jnp.int32)]

    theirs = shift(mine, "tensor", 1)
    lead = min(LEAD, nblocks - 1)
    prev_rows = shift(mine[: lead * tile], "graph", 1)

    def back_terms(ranges, kinds, waits=()):
        return call(
            functools.partial(back_body, ranges, nblocks),
            [*index, grads.reshape(blocks)],
            [(blocks, kind) for kind in kinds],
            work
            + [pltpu.SMEM(x.shape, jnp.int32) for x in index[:3]]
            + [pltpu.VMEM(tiles.shape, BF16), pltpu.VMEM(blocks, BF16), pltpu.SemaphoreType.DMA((5,))],
            cost=BACK_COST,
            space=HBM,
            limit=58,
            waits=waits,
        )

    def tick(cost, *waits):
        return call(tick_body, [], [((8, 128), F32)], cost=cost, waits=waits)[0]

    def triplet(lows, pieces, start, kind, cost):
        return call(
            functools.partial(triplet_body, lows, nblocks),
            [*index, *pieces, start],
            [(blocks, kind)],
            work,
            cost=cost,
        )[0]

    (to_prev,) = back_terms((0,), (BF16,))
    from_next = shift(to_prev, "graph", -1)
    to_next, back = back_terms((2 * nblocks, nblocks), (BF16, F32), [to_prev])
    from_prev = shift(to_next, "graph", 1)
    cuts = [0, min(FIRST, nblocks - 1), nblocks]
    sizes = [nblocks - lead] + [high - low for low, high in zip(cuts, cuts[1:])]
    act, factor, flipped, *sent = call(
        functools.partial(preact_body, 256),
        [mine, theirs, weight],
        [(flat, BF16), (flat, F32), ((depth, rows), BF16)] + [((n * tile, chans), BF16) for n in sizes],
        cost=PREACT_COST,
    )
    up, first, second = [x.reshape(-1, tile, chans) for x in sent]
    prev_high = shift(up, "graph", 1)
    (prev_low,) = call(
        activate_body,
        [prev_rows, shift(prev_rows, "tensor", 1), weight],
        [((lead * tile, chans), BF16)],
        cost=PREACT_COST,
    )
    prev_low = prev_low.reshape(lead, tile, chans)
    others = partners()
    size = depth // (len(others) + 1)
    part = ((size, chans), BF16)
    to_core, gsum, keep, *sends, first = call(
        functools.partial(slope_body, 256),
        [back.reshape(flat), from_next.reshape(flat), from_prev.reshape(flat), factor, grads, weight, flipped],
        [(flat, BF16), (flat, F32), ((size, chans), F32)] + [part] * len(others),
        [pltpu.VMEM(flat, BF16), pltpu.VMEM((depth, chans), F32)],
        cost=SLOPE_COST,
        waits=[prev_low],
        carried=[first],
    )
    arrived = [to_partner(s, *at) for s, at in zip(sends, others)]
    next_first = shift(first, "graph", -1)
    summed = shift(to_core, "tensor", 1)
    grad_edges, token = call(grads_body, [gsum, summed], [(flat, BF16), ((8, 128), F32)], cost=GRADS_COST)
    acc = triplet((0, nblocks), (prev_low, act.reshape(blocks)), mine.reshape(blocks), F32, TRIPLET_COSTS[0])
    scale = float(1.0 / (ndp * edges_in.shape[0] * nz * rows) ** 0.5)
    stages = bits(nz)
    total, second = call(
        functools.partial(total_body, 1.0 if stages else scale),
        [keep, *arrived],
        [part],
        cost=SUM_COST,
        waits=[acc, tick(TICK_COSTS[0], prev_high)],
        carried=[second],
    )
    next_second = shift(second, "graph", -1)
    acc = triplet((lead,), (prev_high,), acc, F32, TRIPLET_COSTS[1])
    waits = [token, acc, tick(TICK_COSTS[1], next_first)]
    for bit in stages:
        (total,) = call(
            functools.partial(total_body, scale if bit == stages[-1] else 1.0),
            [total, swap(total, bit)],
            [part],
            cost=SUM_COST,
            waits=waits,
        )
    arrived = [to_partner(total, *at) for at in others]
    acc = triplet((2 * nblocks,), (next_first,), acc, F32, TRIPLET_COSTS[2])
    (grad_weight,) = call(
        gather_body,
        [total, *arrived],
        [((depth, chans), F32)],
        cost=GATHER_COST,
    )
    edges_out = triplet((2 * nblocks + cuts[1],), (next_second,), acc, BF16, TRIPLET_COSTS[3])
    return edges_out.reshape(1, rows, chans), grad_edges[None], grad_weight


def solution(mesh):
    placed = (
        P(("parts", "dp"), "graph", "tensor"),
        P(None, "tensor"),
        P(("parts", "dp"), "graph", None, None),
        P(("parts", "dp"), "graph"),
        P(("parts", "dp"), "graph"),
        P(("parts", "dp"), "graph"),
        P(("parts", "dp"), "graph", "tensor"),
    )
    return jax.shard_map(
        shards,
        mesh=mesh,
        in_specs=placed,
        out_specs=(
            P(("parts", "dp"), "graph", "tensor"),
            P(("parts", "dp"), "graph", "tensor"),
            P("parts", "tensor"),
        ),
        check_vma=False,
    )
```

```python
import functools

import jax
import jax.numpy as jnp
from jax import lax
from jax.experimental import pallas as pl
from jax.experimental.pallas import tpu as pltpu
from jax.sharding import PartitionSpec as P

F32 = jnp.float32
BF16 = jnp.bfloat16
UNROLL = 4
LEAD = 4
FIRST = 4
BACK_COST, PREACT_COST, SLOPE_COST, SUM_COST, GATHER_COST, GRADS_COST = 1.0, 1.0, 0.5, 2.0, 3.0, 0.5
TICK_COSTS = (3.0, 0.3)
TRIPLET_COSTS = (0.5, 0.3, 0.3, 6.0)
VMEM = pl.BlockSpec(memory_space=pltpu.VMEM)
SMEM = pl.BlockSpec(memory_space=pltpu.SMEM)
HBM = pl.BlockSpec(memory_space=pltpu.HBM)
ANY = pl.BlockSpec(memory_space=pl.ANY)


def call(body, ins, outs, scratch=(), cost=0.0, space=None, limit=32, waits=(), carried=()):
    n, extra = len(ins), len(waits) + len(carried)

    def kernel(*refs):
        results = refs[n + extra :]
        body(*refs[:n], *results[: len(outs)], *results[len(outs) + len(carried) :])

    return pl.pallas_call(
        kernel,
        name=getattr(body, "func", body).__name__,
        in_specs=[space or (SMEM if x.dtype == jnp.int32 else VMEM) for x in ins] + [ANY] * extra,
        out_shape=[jax.ShapeDtypeStruct(s, d) for s, d in outs]
        + [jax.ShapeDtypeStruct(x.shape, x.dtype) for x in carried],
        out_specs=[VMEM for _ in outs] + [ANY for _ in carried],
        scratch_shapes=list(scratch),
        input_output_aliases={n + len(waits) + i: len(outs) + i for i in range(len(carried))},
        cost_estimate=pl.CostEstimate(flops=int(cost * 1.15e9), bytes_accessed=0, transcendentals=0),
        compiler_params=pltpu.CompilerParams(vmem_limit_bytes=limit * 1024 * 1024),
    )(*ins, *waits, *carried)


def shift(value, axis, steps):
    count = lax.axis_size(axis)
    return lax.ppermute(value, axis, [(i, (i + steps) % count) for i in range(count)])


def pick(listed, count, source, low, high):
    slots = source.shape[1]

    found = jnp.int32(0)
    for k in range(slots):
        listed[found] = k
        s = source[0, k]
        inside = (k < count) & (s >= low) & (s < high)
        found = found + inside.astype(jnp.int32)
    for j in range(UNROLL):
        listed[found + j] = 0
    return found


def over_tiles(listed, found, step):
    def some(i, carry):
        for j in range(UNROLL):
            at = i * UNROLL + j
            step(listed[at], at < found)
        return carry

    lax.fori_loop(0, (found + UNROLL - 1) // UNROLL, some, 0)


def back_body(ranges, nblocks, counts_hbm, target_hbm, source_hbm, tiles_hbm, grads_hbm, *rest):
    n = len(ranges)
    outs = rest[:n]
    acc, listed, counts, target, source, tiles, grads, sems = rest[n:]
    copies = [
        pltpu.make_async_copy(there, here, sems.at[i])
        for i, (there, here) in enumerate(
            [
                (counts_hbm, counts),
                (source_hbm, source),
                (target_hbm, target),
                (grads_hbm, grads),
                (tiles_hbm, tiles),
            ]
        )
    ]
    for copy in copies:
        copy.start()
    acc[...] = jnp.zeros_like(acc)
    for copy in copies[:3]:
        copy.wait()
    for low, out in zip(ranges, outs):
        if low != ranges[0]:
            acc[...] = jnp.zeros_like(acc)
        found = pick(listed, counts[0, 0], source, low, low + nblocks)
        if low == ranges[0]:
            for copy in copies[3:]:
                copy.wait()

        def step(k, valid):
            at = jnp.where(valid, source[0, k] - low, nblocks)
            acc[at] += lax.dot_general(
                tiles[k], grads[target[0, k]], (((0,), (0,)), ((), ())), preferred_element_type=F32
            )

        over_tiles(listed, found, step)
        for b in range(nblocks):
            out[b] = acc[b].astype(out.dtype)


def triplet_body(lows, nblocks, counts, target, source, tiles, *rest):
    n = len(lows)
    rows, start, out, acc, listed = rest[:n], *rest[n:]
    for b in range(nblocks):
        acc[b] = start[b].astype(F32)
    for low, piece in zip(lows, rows):
        found = pick(listed, counts[0, 0], source, low, low + piece.shape[0])

        def step(k, valid):
            at = jnp.where(valid, target[0, k], nblocks)
            s = jnp.where(valid, source[0, k] - low, 0)
            acc[at] += jnp.dot(tiles[k], piece[s], preferred_element_type=F32)

        over_tiles(listed, found, step)
    for b in range(nblocks):
        out[b] = acc[b].astype(out.dtype)


def preact_body(step, mine, theirs, weight, act, factor, flipped, up, *down):
    rows, chans = mine.shape
    core = lax.axis_index("tensor")
    own = pl.ds(pl.multiple_of(core * chans, chans), chans)
    other = pl.ds(pl.multiple_of((1 - core) * chans, chans), chans)
    for r in range(0, rows, step):
        at = pl.ds(r, step)
        pre = jnp.dot(mine[at], weight[own], preferred_element_type=F32) + jnp.dot(
            theirs[at], weight[other], preferred_element_type=F32
        )
        sig = 1.0 / (1.0 + jnp.exp(-pre))
        act[at] = (pre * sig).astype(BF16)
        factor[at] = sig * (1.0 + pre * (1.0 - sig))
        flipped[own, at] = mine[at].T
        flipped[other, at] = theirs[at].T
    up[...] = act[pl.ds(rows - up.shape[0], up.shape[0])]
    begin = 0
    for piece in down:
        piece[...] = act[pl.ds(begin, piece.shape[0])]
        begin += piece.shape[0]


def tick_body(out):
    out[...] = jnp.zeros_like(out)


def activate_body(mine, theirs, weight, act):
    chans = mine.shape[1]
    core = lax.axis_index("tensor")
    own = pl.ds(pl.multiple_of(core * chans, chans), chans)
    other = pl.ds(pl.multiple_of((1 - core) * chans, chans), chans)
    pre = jnp.dot(mine[...], weight[own], preferred_element_type=F32) + jnp.dot(
        theirs[...], weight[other], preferred_element_type=F32
    )
    act[...] = (pre / (1.0 + jnp.exp(-pre))).astype(BF16)


def partners():
    return [(f, d) for f in (0, 1) for d in range(lax.axis_size("dp")) if (f, d) != (0, 0)]


def to_partner(value, flip, steps):
    nz, ndp = lax.axis_size("graph"), lax.axis_size("dp")
    pairs = [
        (z * ndp + d, (z ^ flip) * ndp + (d + steps) % ndp) for z in range(nz) for d in range(ndp)
    ]
    return lax.ppermute(value, ("graph", "dp"), pairs)


def swap(value, bit):
    return lax.ppermute(value, "graph", [(z, z ^ bit) for z in range(lax.axis_size("graph"))])


def place(flip, steps, size):
    ndp = lax.axis_size("dp")
    d = lax.rem(lax.axis_index("dp") + steps + ndp, ndp)
    b = lax.rem(lax.axis_index("graph") + flip, 2)
    return pl.ds(pl.multiple_of((d * 2 + b) * size, size), size)


def slope_body(step, back, from_next, from_prev, factor, grads, weight, flipped, *rest):
    to_core, gsum, keep = rest[:3]
    others = partners()
    sends = rest[3 : 3 + len(others)]
    slope, part = rest[3 + len(others) :]
    rows, chans = grads.shape
    core = lax.axis_index("tensor")
    own = pl.ds(pl.multiple_of(core * chans, chans), chans)
    other = pl.ds(pl.multiple_of((1 - core) * chans, chans), chans)
    last = (((1,), (1,)), ((), ()))
    for r in range(0, rows, step):
        at = pl.ds(r, step)
        total = back[at] + from_next[at].astype(F32) + from_prev[at].astype(F32)
        piece = (total * factor[at]).astype(BF16)
        slope[at] = piece
        to_core[at] = lax.dot_general(piece, weight[other], last, preferred_element_type=F32).astype(BF16)
        gsum[at] = grads[at].astype(F32) + lax.dot_general(
            piece, weight[own], last, preferred_element_type=F32
        )
    part[...] = jnp.dot(flipped[...], slope[...], preferred_element_type=F32)
    size = keep.shape[0]
    keep[...] = part[place(0, 0, size)]
    for (flip, steps), send in zip(others, sends):
        send[...] = part[place(flip, steps, size)].astype(BF16)


def grads_body(gsum, arrived, out, token):
    token[...] = jnp.zeros_like(token)
    out[...] = (gsum[...] + arrived[...].astype(F32)).astype(BF16)


def total_body(scale, *refs):
    total = refs[0][...].astype(F32)
    for ref in refs[1:-1]:
        total = total + ref[...].astype(F32)
    refs[-1][...] = (total * scale).astype(BF16)


def gather_body(mine, *rest):
    out = rest[-1]
    size = mine.shape[0]
    out[place(0, 0, size)] = mine[...].astype(F32)
    for (flip, steps), ref in zip(partners(), rest):
        out[place(flip, -steps, size)] = ref[...].astype(F32)


def bits(nz):
    return [1 << i for i in range(1, nz.bit_length() - 1)]


def shards(edges_in, weight, basis_tiles, target_blocks, source_blocks, counts, grad_out):
    rows, chans = edges_in.shape[1], edges_in.shape[2]
    tile = basis_tiles.shape[2]
    nblocks = rows // tile
    slots = basis_tiles.shape[1]
    depth = weight.shape[0]
    ndp, nz = lax.axis_size("dp"), lax.axis_size("graph")
    mine, grads, tiles = edges_in[0], grad_out[0], basis_tiles[0]
    blocks = (nblocks, tile, chans)
    flat = (rows, chans)
    index = [counts, target_blocks, source_blocks, tiles]
    work = [pltpu.VMEM((nblocks + 1, tile, chans), F32), pltpu.SMEM((slots + UNROLL,), jnp.int32)]

    theirs = shift(mine, "tensor", 1)
    lead = min(LEAD, nblocks - 1)
    prev_rows = shift(mine[: lead * tile], "graph", 1)

    def back_terms(ranges, kinds, waits=()):
        return call(
            functools.partial(back_body, ranges, nblocks),
            [*index, grads.reshape(blocks)],
            [(blocks, kind) for kind in kinds],
            work
            + [pltpu.SMEM(x.shape, jnp.int32) for x in index[:3]]
            + [pltpu.VMEM(tiles.shape, BF16), pltpu.VMEM(blocks, BF16), pltpu.SemaphoreType.DMA((5,))],
            cost=BACK_COST,
            space=HBM,
            limit=58,
            waits=waits,
        )

    def tick(cost, *waits):
        return call(tick_body, [], [((8, 128), F32)], cost=cost, waits=waits)[0]

    def triplet(lows, pieces, start, kind, cost):
        return call(
            functools.partial(triplet_body, lows, nblocks),
            [*index, *pieces, start],
            [(blocks, kind)],
            work,
            cost=cost,
        )[0]

    (to_prev,) = back_terms((0,), (BF16,))
    from_next = shift(to_prev, "graph", -1)
    to_next, back = back_terms((2 * nblocks, nblocks), (BF16, F32), [to_prev])
    from_prev = shift(to_next, "graph", 1)
    cuts = [0, min(FIRST, nblocks - 1), nblocks]
    sizes = [nblocks - lead] + [high - low for low, high in zip(cuts, cuts[1:])]
    act, factor, flipped, *sent = call(
        functools.partial(preact_body, 256),
        [mine, theirs, weight],
        [(flat, BF16), (flat, F32), ((depth, rows), BF16)] + [((n * tile, chans), BF16) for n in sizes],
        cost=PREACT_COST,
    )
    up, first, second = [x.reshape(-1, tile, chans) for x in sent]
    prev_high = shift(up, "graph", 1)
    (prev_low,) = call(
        activate_body,
        [prev_rows, shift(prev_rows, "tensor", 1), weight],
        [((lead * tile, chans), BF16)],
        cost=PREACT_COST,
    )
    prev_low = prev_low.reshape(lead, tile, chans)
    others = partners()
    size = depth // (len(others) + 1)
    part = ((size, chans), BF16)
    to_core, gsum, keep, *sends, first = call(
        functools.partial(slope_body, 256),
        [back.reshape(flat), from_next.reshape(flat), from_prev.reshape(flat), factor, grads, weight, flipped],
        [(flat, BF16), (flat, F32), ((size, chans), F32)] + [part] * len(others),
        [pltpu.VMEM(flat, BF16), pltpu.VMEM((depth, chans), F32)],
        cost=SLOPE_COST,
        waits=[prev_low],
        carried=[first],
    )
    arrived = [to_partner(s, *at) for s, at in zip(sends, others)]
    next_first = shift(first, "graph", -1)
    summed = shift(to_core, "tensor", 1)
    grad_edges, token = call(grads_body, [gsum, summed], [(flat, BF16), ((8, 128), F32)], cost=GRADS_COST)
    acc = triplet((0, nblocks), (prev_low, act.reshape(blocks)), mine.reshape(blocks), F32, TRIPLET_COSTS[0])
    scale = float(1.0 / (ndp * edges_in.shape[0] * nz * rows) ** 0.5)
    stages = bits(nz)
    total, second = call(
        functools.partial(total_body, 1.0 if stages else scale),
        [keep, *arrived],
        [part],
        cost=SUM_COST,
        waits=[acc, tick(TICK_COSTS[0], prev_high)],
        carried=[second],
    )
    next_second = shift(second, "graph", -1)
    acc = triplet((lead,), (prev_high,), acc, F32, TRIPLET_COSTS[1])
    waits = [token, acc, tick(TICK_COSTS[1], next_first)]
    for bit in stages:
        (total,) = call(
            functools.partial(total_body, scale if bit == stages[-1] else 1.0),
            [total, swap(total, bit)],
            [part],
            cost=SUM_COST,
            waits=waits,
        )
    arrived = [to_partner(total, *at) for at in others]
    acc = triplet((2 * nblocks,), (next_first,), acc, F32, TRIPLET_COSTS[2])
    (grad_weight,) = call(
        gather_body,
        [total, *arrived],
        [((depth, chans), F32)],
        cost=GATHER_COST,
    )
    edges_out = triplet((2 * nblocks + cuts[1],), (next_second,), acc, BF16, TRIPLET_COSTS[3])
    return edges_out.reshape(1, rows, chans), grad_edges[None], grad_weight


def solution(mesh):
    placed = (
        P(("parts", "dp"), "graph", "tensor"),
        P(None, "tensor"),
        P(("parts", "dp"), "graph", None, None),
        P(("parts", "dp"), "graph"),
        P(("parts", "dp"), "graph"),
        P(("parts", "dp"), "graph"),
        P(("parts", "dp"), "graph", "tensor"),
    )
    return jax.shard_map(
        shards,
        mesh=mesh,
        in_specs=placed,
        out_specs=(
            P(("parts", "dp"), "graph", "tensor"),
            P(("parts", "dp"), "graph", "tensor"),
            P("parts", "tensor"),
        ),
        check_vma=False,
    )
```

```python
import functools

import jax
import jax.numpy as jnp
from jax import lax
from jax.experimental import pallas as pl
from jax.experimental.pallas import tpu as pltpu
from jax.sharding import PartitionSpec as P

F32 = jnp.float32
BF16 = jnp.bfloat16
UNROLL = 4
LEAD = 4
FIRST = 5
BACK_COST, PREACT_COST, SLOPE_COST, SUM_COST, GATHER_COST, GRADS_COST = 1.0, 1.0, 0.5, 2.0, 3.0, 0.5
TICK_COSTS = (3.0, 0.3)
TRIPLET_COSTS = (0.5, 0.3, 0.3, 6.0)
VMEM = pl.BlockSpec(memory_space=pltpu.VMEM)
SMEM = pl.BlockSpec(memory_space=pltpu.SMEM)
HBM = pl.BlockSpec(memory_space=pltpu.HBM)
ANY = pl.BlockSpec(memory_space=pl.ANY)


def call(body, ins, outs, scratch=(), cost=0.0, space=None, limit=32, waits=(), carried=()):
    n, extra = len(ins), len(waits) + len(carried)

    def kernel(*refs):
        results = refs[n + extra :]
        body(*refs[:n], *results[: len(outs)], *results[len(outs) + len(carried) :])

    return pl.pallas_call(
        kernel,
        name=getattr(body, "func", body).__name__,
        in_specs=[space or (SMEM if x.dtype == jnp.int32 else VMEM) for x in ins] + [ANY] * extra,
        out_shape=[jax.ShapeDtypeStruct(s, d) for s, d in outs]
        + [jax.ShapeDtypeStruct(x.shape, x.dtype) for x in carried],
        out_specs=[VMEM for _ in outs] + [ANY for _ in carried],
        scratch_shapes=list(scratch),
        input_output_aliases={n + len(waits) + i: len(outs) + i for i in range(len(carried))},
        cost_estimate=pl.CostEstimate(flops=int(cost * 1.15e9), bytes_accessed=0, transcendentals=0),
        compiler_params=pltpu.CompilerParams(vmem_limit_bytes=limit * 1024 * 1024),
    )(*ins, *waits, *carried)


def shift(value, axis, steps):
    count = lax.axis_size(axis)
    return lax.ppermute(value, axis, [(i, (i + steps) % count) for i in range(count)])


def pick(listed, count, source, low, high):
    slots = source.shape[1]

    found = jnp.int32(0)
    for k in range(slots):
        listed[found] = k
        s = source[0, k]
        inside = (k < count) & (s >= low) & (s < high)
        found = found + inside.astype(jnp.int32)
    for j in range(UNROLL):
        listed[found + j] = 0
    return found


def over_tiles(listed, found, step):
    def some(i, carry):
        for j in range(UNROLL):
            at = i * UNROLL + j
            step(listed[at], at < found)
        return carry

    lax.fori_loop(0, (found + UNROLL - 1) // UNROLL, some, 0)


def back_body(ranges, nblocks, counts_hbm, target_hbm, source_hbm, tiles_hbm, grads_hbm, *rest):
    n = len(ranges)
    outs = rest[:n]
    acc, listed, counts, target, source, tiles, grads, sems = rest[n:]
    copies = [
        pltpu.make_async_copy(there, here, sems.at[i])
        for i, (there, here) in enumerate(
            [
                (counts_hbm, counts),
                (source_hbm, source),
                (target_hbm, target),
                (grads_hbm, grads),
                (tiles_hbm, tiles),
            ]
        )
    ]
    for copy in copies:
        copy.start()
    acc[...] = jnp.zeros_like(acc)
    for copy in copies[:3]:
        copy.wait()
    for low, out in zip(ranges, outs):
        if low != ranges[0]:
            acc[...] = jnp.zeros_like(acc)
        found = pick(listed, counts[0, 0], source, low, low + nblocks)
        if low == ranges[0]:
            for copy in copies[3:]:
                copy.wait()

        def step(k, valid):
            at = jnp.where(valid, source[0, k] - low, nblocks)
            acc[at] += lax.dot_general(
                tiles[k], grads[target[0, k]], (((0,), (0,)), ((), ())), preferred_element_type=F32
            )

        over_tiles(listed, found, step)
        for b in range(nblocks):
            out[b] = acc[b].astype(out.dtype)


def triplet_body(lows, nblocks, counts, target, source, tiles, *rest):
    n = len(lows)
    rows, start, out, acc, listed = rest[:n], *rest[n:]
    for b in range(nblocks):
        acc[b] = start[b].astype(F32)
    for low, piece in zip(lows, rows):
        found = pick(listed, counts[0, 0], source, low, low + piece.shape[0])

        def step(k, valid):
            at = jnp.where(valid, target[0, k], nblocks)
            s = jnp.where(valid, source[0, k] - low, 0)
            acc[at] += jnp.dot(tiles[k], piece[s], preferred_element_type=F32)

        over_tiles(listed, found, step)
    for b in range(nblocks):
        out[b] = acc[b].astype(out.dtype)


def preact_body(step, mine, theirs, weight, act, factor, flipped, up, *down):
    rows, chans = mine.shape
    core = lax.axis_index("tensor")
    own = pl.ds(pl.multiple_of(core * chans, chans), chans)
    other = pl.ds(pl.multiple_of((1 - core) * chans, chans), chans)
    for r in range(0, rows, step):
        at = pl.ds(r, step)
        pre = jnp.dot(mine[at], weight[own], preferred_element_type=F32) + jnp.dot(
            theirs[at], weight[other], preferred_element_type=F32
        )
        sig = 1.0 / (1.0 + jnp.exp(-pre))
        act[at] = (pre * sig).astype(BF16)
        factor[at] = sig * (1.0 + pre * (1.0 - sig))
        flipped[own, at] = mine[at].T
        flipped[other, at] = theirs[at].T
    up[...] = act[pl.ds(rows - up.shape[0], up.shape[0])]
    begin = 0
    for piece in down:
        piece[...] = act[pl.ds(begin, piece.shape[0])]
        begin += piece.shape[0]


def tick_body(out):
    out[...] = jnp.zeros_like(out)


def activate_body(mine, theirs, weight, act):
    chans = mine.shape[1]
    core = lax.axis_index("tensor")
    own = pl.ds(pl.multiple_of(core * chans, chans), chans)
    other = pl.ds(pl.multiple_of((1 - core) * chans, chans), chans)
    pre = jnp.dot(mine[...], weight[own], preferred_element_type=F32) + jnp.dot(
        theirs[...], weight[other], preferred_element_type=F32
    )
    act[...] = (pre / (1.0 + jnp.exp(-pre))).astype(BF16)


def partners():
    return [(f, d) for f in (0, 1) for d in range(lax.axis_size("dp")) if (f, d) != (0, 0)]


def to_partner(value, flip, steps):
    nz, ndp = lax.axis_size("graph"), lax.axis_size("dp")
    pairs = [
        (z * ndp + d, (z ^ flip) * ndp + (d + steps) % ndp) for z in range(nz) for d in range(ndp)
    ]
    return lax.ppermute(value, ("graph", "dp"), pairs)


def swap(value, bit):
    return lax.ppermute(value, "graph", [(z, z ^ bit) for z in range(lax.axis_size("graph"))])


def place(flip, steps, size):
    ndp = lax.axis_size("dp")
    d = lax.rem(lax.axis_index("dp") + steps + ndp, ndp)
    b = lax.rem(lax.axis_index("graph") + flip, 2)
    return pl.ds(pl.multiple_of((d * 2 + b) * size, size), size)


def slope_body(step, back, from_next, from_prev, factor, grads, weight, flipped, *rest):
    to_core, gsum, keep = rest[:3]
    others = partners()
    sends = rest[3 : 3 + len(others)]
    slope, part = rest[3 + len(others) :]
    rows, chans = grads.shape
    core = lax.axis_index("tensor")
    own = pl.ds(pl.multiple_of(core * chans, chans), chans)
    other = pl.ds(pl.multiple_of((1 - core) * chans, chans), chans)
    last = (((1,), (1,)), ((), ()))
    for r in range(0, rows, step):
        at = pl.ds(r, step)
        total = back[at] + from_next[at].astype(F32) + from_prev[at].astype(F32)
        piece = (total * factor[at]).astype(BF16)
        slope[at] = piece
        to_core[at] = lax.dot_general(piece, weight[other], last, preferred_element_type=F32).astype(BF16)
        gsum[at] = grads[at].astype(F32) + lax.dot_general(
            piece, weight[own], last, preferred_element_type=F32
        )
    part[...] = jnp.dot(flipped[...], slope[...], preferred_element_type=F32)
    size = keep.shape[0]
    keep[...] = part[place(0, 0, size)]
    for (flip, steps), send in zip(others, sends):
        send[...] = part[place(flip, steps, size)].astype(BF16)


def grads_body(gsum, arrived, out, token):
    token[...] = jnp.zeros_like(token)
    out[...] = (gsum[...] + arrived[...].astype(F32)).astype(BF16)


def total_body(scale, *refs):
    total = refs[0][...].astype(F32)
    for ref in refs[1:-1]:
        total = total + ref[...].astype(F32)
    refs[-1][...] = (total * scale).astype(BF16)


def gather_body(mine, *rest):
    out = rest[-1]
    size = mine.shape[0]
    out[place(0, 0, size)] = mine[...].astype(F32)
    for (flip, steps), ref in zip(partners(), rest):
        out[place(flip, -steps, size)] = ref[...].astype(F32)


def bits(nz):
    return [1 << i for i in range(1, nz.bit_length() - 1)]


def shards(edges_in, weight, basis_tiles, target_blocks, source_blocks, counts, grad_out):
    rows, chans = edges_in.shape[1], edges_in.shape[2]
    tile = basis_tiles.shape[2]
    nblocks = rows // tile
    slots = basis_tiles.shape[1]
    depth = weight.shape[0]
    ndp, nz = lax.axis_size("dp"), lax.axis_size("graph")
    mine, grads, tiles = edges_in[0], grad_out[0], basis_tiles[0]
    blocks = (nblocks, tile, chans)
    flat = (rows, chans)
    index = [counts, target_blocks, source_blocks, tiles]
    work = [pltpu.VMEM((nblocks + 1, tile, chans), F32), pltpu.SMEM((slots + UNROLL,), jnp.int32)]

    theirs = shift(mine, "tensor", 1)
    lead = min(LEAD, nblocks - 1)
    prev_rows = shift(mine[: lead * tile], "graph", 1)

    def back_terms(ranges, kinds, waits=()):
        return call(
            functools.partial(back_body, ranges, nblocks),
            [*index, grads.reshape(blocks)],
            [(blocks, kind) for kind in kinds],
            work
            + [pltpu.SMEM(x.shape, jnp.int32) for x in index[:3]]
            + [pltpu.VMEM(tiles.shape, BF16), pltpu.VMEM(blocks, BF16), pltpu.SemaphoreType.DMA((5,))],
            cost=BACK_COST,
            space=HBM,
            limit=58,
            waits=waits,
        )

    def tick(cost, *waits):
        return call(tick_body, [], [((8, 128), F32)], cost=cost, waits=waits)[0]

    def triplet(lows, pieces, start, kind, cost):
        return call(
            functools.partial(triplet_body, lows, nblocks),
            [*index, *pieces, start],
            [(blocks, kind)],
            work,
            cost=cost,
        )[0]

    (to_prev,) = back_terms((0,), (BF16,))
    from_next = shift(to_prev, "graph", -1)
    to_next, back = back_terms((2 * nblocks, nblocks), (BF16, F32), [to_prev])
    from_prev = shift(to_next, "graph", 1)
    cuts = [0, min(FIRST, nblocks - 1), nblocks]
    sizes = [nblocks - lead] + [high - low for low, high in zip(cuts, cuts[1:])]
    act, factor, flipped, *sent = call(
        functools.partial(preact_body, 256),
        [mine, theirs, weight],
        [(flat, BF16), (flat, F32), ((depth, rows), BF16)] + [((n * tile, chans), BF16) for n in sizes],
        cost=PREACT_COST,
    )
    up, first, second = [x.reshape(-1, tile, chans) for x in sent]
    prev_high = shift(up, "graph", 1)
    (prev_low,) = call(
        activate_body,
        [prev_rows, shift(prev_rows, "tensor", 1), weight],
        [((lead * tile, chans), BF16)],
        cost=PREACT_COST,
    )
    prev_low = prev_low.reshape(lead, tile, chans)
    others = partners()
    size = depth // (len(others) + 1)
    part = ((size, chans), BF16)
    to_core, gsum, keep, *sends, first = call(
        functools.partial(slope_body, 256),
        [back.reshape(flat), from_next.reshape(flat), from_prev.reshape(flat), factor, grads, weight, flipped],
        [(flat, BF16), (flat, F32), ((size, chans), F32)] + [part] * len(others),
        [pltpu.VMEM(flat, BF16), pltpu.VMEM((depth, chans), F32)],
        cost=SLOPE_COST,
        waits=[prev_low],
        carried=[first],
    )
    arrived = [to_partner(s, *at) for s, at in zip(sends, others)]
    next_first = shift(first, "graph", -1)
    summed = shift(to_core, "tensor", 1)
    grad_edges, token = call(grads_body, [gsum, summed], [(flat, BF16), ((8, 128), F32)], cost=GRADS_COST)
    acc = triplet((0, nblocks), (prev_low, act.reshape(blocks)), mine.reshape(blocks), F32, TRIPLET_COSTS[0])
    scale = float(1.0 / (ndp * edges_in.shape[0] * nz * rows) ** 0.5)
    stages = bits(nz)
    total, second = call(
        functools.partial(total_body, 1.0 if stages else scale),
        [keep, *arrived],
        [part],
        cost=SUM_COST,
        waits=[acc, tick(TICK_COSTS[0], prev_high)],
        carried=[second],
    )
    next_second = shift(second, "graph", -1)
    acc = triplet((lead,), (prev_high,), acc, F32, TRIPLET_COSTS[1])
    waits = [token, acc, tick(TICK_COSTS[1], next_first)]
    for bit in stages:
        (total,) = call(
            functools.partial(total_body, scale if bit == stages[-1] else 1.0),
            [total, swap(total, bit)],
            [part],
            cost=SUM_COST,
            waits=waits,
        )
    arrived = [to_partner(total, *at) for at in others]
    acc = triplet((2 * nblocks,), (next_first,), acc, F32, TRIPLET_COSTS[2])
    (grad_weight,) = call(
        gather_body,
        [total, *arrived],
        [((depth, chans), F32)],
        cost=GATHER_COST,
    )
    edges_out = triplet((2 * nblocks + cuts[1],), (next_second,), acc, BF16, TRIPLET_COSTS[3])
    return edges_out.reshape(1, rows, chans), grad_edges[None], grad_weight


def solution(mesh):
    placed = (
        P(("parts", "dp"), "graph", "tensor"),
        P(None, "tensor"),
        P(("parts", "dp"), "graph", None, None),
        P(("parts", "dp"), "graph"),
        P(("parts", "dp"), "graph"),
        P(("parts", "dp"), "graph"),
        P(("parts", "dp"), "graph", "tensor"),
    )
    return jax.shard_map(
        shards,
        mesh=mesh,
        in_specs=placed,
        out_specs=(
            P(("parts", "dp"), "graph", "tensor"),
            P(("parts", "dp"), "graph", "tensor"),
            P("parts", "tensor"),
        ),
        check_vma=False,
    )
```
